256 devices in a mesh: wide: 64 (over z, x, y_hi), narrow: 4 (over y_lo, core).
Axes of the slice: x: 4, y: 4 (y_hi: 2, y_lo: 2; y = y_hi * 2 + y_lo), z: 8, core: 2. Of those that a mesh axis runs over, the one named last changes fastest.
Arguments:
- waveforms: bfloat16 [512, 12, 16384], P('wide', None, 'narrow'), may hold values from -122 to 122
- templates: bfloat16 [512, 12, 300], P('wide'), may hold values from -15 to 15
- det_station: int32 [512, 64], P('wide', 'narrow'), may hold values from 0 to 511, as said below
- det_block: int32 [512, 64], P('wide', 'narrow'), may hold values from 0 to 124, as said below
- det_count: int32 [512], P('wide'), may hold values from 1 to 64, 20480 in all
Outputs:
- detections: float32 [512, 64, 128], P('wide', 'narrow')
The draws below stay inside these ranges and needn't reach their ends.
Inputs may be any that keep to these rules, and one draw needn't show every extreme that they name: `det_station`: in the slots of one device (one index of wide's templates, row slots of one part of the hour), at most 4 rows name stations s of one value of s // 8; exactly 4 do for one such value, the same one for every device of a part of the hour; padding rows included. `det_block`: row slot r names a block of part p = r // 16 of the hour, 4096 // 128 * p or later and before 4096 // 128 * (p + 1); every named block's windows end inside the hour. Rows from det_count on are padding.
All inputs are finite; a program needn't handle non-finite values. No bound on the sum of `det_count` on one device may be relied on, other than what follows from the above.
Results may differ from the reference program's by a relative error of at most 0.003.
Values may be sent and summed in bfloat16 or wider, within the bound.
No kernel may reach another device: no remote copies, remote signals or barrier semaphores. Data moves between devices by JAX's collectives and lax.ppermute only.
A program may use at most 128 MiB of HBM per device.

```python
import math
import jax
import jax.numpy as jnp
import numpy as np
from jax import lax

CH = 12
L = 300
BLK = 128
ROWS_PART = 16
STA_DEV = 8
TPL_DEV = 8
SEG = 4096
STATIONS = 512
TEMPLATES = 512
NT = 16384
ROWS = 64
NBLK = 125
CAP = 4


def draw_waveforms(key, part):
    keys = jax.random.split(jax.random.fold_in(key, 11), 4)
    groups = NT // 16
    envelope = jnp.exp(jax.random.uniform(keys[1], (STATIONS, CH, groups, 1), jnp.float32, 0.0, math.log(10.0)))
    channel_gain = jnp.exp(jax.random.uniform(keys[2], (STATIONS, CH, 1, 1), jnp.float32, 0.0, math.log(3.0)))
    offset = 2.0 * jax.random.uniform(keys[3], (STATIONS, CH, groups, 1), jnp.float32, -1.0, 1.0)
    noise = jnp.clip(jax.random.normal(keys[0], (STATIONS, CH, groups, 16), jnp.float32), -4.0, 4.0)
    return (noise * envelope * channel_gain + offset).reshape(STATIONS, CH, NT).astype(jnp.bfloat16)


def draw_templates(key, part):
    keys = jax.random.split(jax.random.fold_in(key, 23), 3)
    scale = jnp.exp(jax.random.uniform(keys[1], (TEMPLATES, CH, 1), jnp.float32, math.log(0.3), math.log(3.0)))
    offset = jax.random.uniform(keys[2], (TEMPLATES, CH, 1), jnp.float32, -1.0, 1.0)
    shape_part = jnp.clip(jax.random.normal(keys[0], (TEMPLATES, CH, L), jnp.float32), -4.0, 4.0)
    return ((shape_part + offset) * scale).astype(jnp.bfloat16)


def draw_det_station(key, part):
    owners = TEMPLATES // TPL_DEV
    parts = ROWS // ROWS_PART
    row_total = TPL_DEV * ROWS_PART
    base = jax.random.fold_in(key, 31)
    hot = jax.random.randint(jax.random.fold_in(base, 1), (parts,), 0, owners)
    pool_index = jnp.arange((owners - 1) * CAP, dtype=jnp.int32) // CAP
    second = jax.random.fold_in(base, 2)

    def one_block(number, hot_one):
        block_key = jax.random.fold_in(second, number)
        keys = jax.random.split(block_key, 3)
        pool = pool_index + (pool_index >= hot_one).astype(jnp.int32)
        chosen = jax.random.permutation(keys[0], pool)[:row_total - CAP]
        holders = jnp.concatenate([jnp.zeros((CAP,), jnp.int32) + hot_one, chosen])
        holders = jax.random.permutation(keys[1], holders)
        within = jax.random.randint(keys[2], (row_total,), 0, STA_DEV)
        return holders * STA_DEV + within
    numbers = jnp.arange(owners * parts, dtype=jnp.int32)
    stations = jax.vmap(one_block)(numbers, hot[numbers % parts])
    stations = stations.reshape(owners, parts, TPL_DEV, ROWS_PART)
    return jnp.transpose(stations, (0, 2, 1, 3)).reshape(TEMPLATES, ROWS)


def draw_det_block(key, part):
    seg_blocks = SEG // BLK
    part_of = jnp.arange(ROWS, dtype=jnp.int32) // ROWS_PART
    highest = jnp.minimum(seg_blocks, NBLK - part_of * seg_blocks)
    offset = jax.random.randint(jax.random.fold_in(key, 41), (TEMPLATES, ROWS), 0, highest[None, :])
    return part_of[None, :] * seg_blocks + offset


def length_profile(count, total, most, skew):
    portions = [(1 << 20) // math.isqrt(grade ** skew) + 1 for grade in range(2, count + 1)]
    rest, given = total - most - (count - 1), [1] * (count - 1)
    while rest > 0:
        free = [i for i in range(count - 1) if given[i] < most]
        whole, budget = sum([portions[i] for i in free]), rest
        for i in free:
            more = min(most - given[i], max(1, budget * portions[i] // whole), rest)
            given[i] = given[i] + more
            rest = rest - more
    return np.array([most] + given)


def ragged_sizes(rng, number_of, total, limit, lean):
    if number_of == 2:
        one = jax.random.randint(rng, (), max(1, total - limit), min(limit, total - 1) + 1)
        return jnp.stack([one, total - one])
    tallies = jnp.asarray(length_profile(number_of, total, limit, lean), jnp.int32)
    couples = (number_of - 1) // 2
    giver, receiver = tallies[1:1 + 2 * couples:2], tallies[2:2 + 2 * couples:2]
    slack = jnp.minimum(giver - 1, limit - receiver)
    moved = jax.random.randint(jax.random.fold_in(rng, 1), (couples,), 0, 1 << 20) % (slack + 1)
    tallies = tallies.at[1:1 + 2 * couples:2].set(giver - moved).at[2:2 + 2 * couples:2].set(receiver + moved)
    return tallies[jax.random.permutation(jax.random.fold_in(rng, 2), number_of)]


def setup_inputs(seed: int = 0) -> dict:
    streams_of = jax.random.split(jax.random.key(seed), 6)
    return {
        "waveforms": draw_waveforms(jax.random.fold_in(streams_of[5], 71), 0),
        "templates": draw_templates(jax.random.fold_in(streams_of[5], 71), 0),
        "det_station": draw_det_station(jax.random.fold_in(streams_of[5], 71), 0),
        "det_block": draw_det_block(jax.random.fold_in(streams_of[5], 71), 0),
        "det_count": ragged_sizes(streams_of[4], TEMPLATES, TEMPLATES * ROWS * 5 // 8, ROWS, 1).astype(jnp.int32),
    }


EPS = 1e-06

def prepare(templates):
    values = templates.astype(jnp.float32)
    centred = values - lax.optimization_barrier(jnp.mean(values, axis=2, keepdims=True))
    template_scale = jnp.sqrt(lax.optimization_barrier(jnp.mean(centred * centred, axis=2)) + EPS)
    return (centred.astype(jnp.bfloat16), template_scale)

def window_scores(windows, kernel, template_scale):
    shifted = jnp.arange(BLK + L - 1)[:, None] - jnp.arange(BLK)[None, :]
    inside = (shifted >= 0) & (shifted < L)
    picked = jnp.clip(shifted, 0, L - 1)
    toeplitz = jnp.where(inside[None, :, :], kernel[:, picked], 0.0)
    band = inside.astype(jnp.float32)
    products = jnp.einsum('rcw,cwi->rci', windows, toeplitz, precision=lax.Precision.HIGHEST)
    first = jnp.einsum('rcw,wi->rci', windows, band, precision=lax.Precision.HIGHEST) / L
    second = jnp.einsum('rcw,wi->rci', windows * windows, band, precision=lax.Precision.HIGHEST) / L
    inverse = 1.0 / jnp.sqrt(second - first * first + EPS)
    weighted = products * inverse / template_scale[None, :, None]
    return math.sqrt(L / CH) / L * lax.optimization_barrier(jnp.sum(weighted, axis=1))

def reference(waveforms, templates, det_station, det_block, det_count):
    rounded, scales = prepare(templates)

    def one_template(bundle):
        kernel, template_scale, stations, blocks, count = bundle

        def one_window(station, block_index):
            return lax.dynamic_slice(waveforms, (station, jnp.int32(0), block_index * BLK), (1, CH, BLK + L - 1))[0]
        windows = jax.vmap(one_window)(stations, blocks)
        scores = window_scores(windows.astype(jnp.float32), kernel.astype(jnp.float32), template_scale)
        in_use = jnp.arange(ROWS) < count
        return jnp.where(in_use[:, None], scores, jnp.float32(0.0))
    return lax.map(one_template, (rounded, scales, det_station, det_block, det_count))
```

```python
import functools

import jax
import jax.numpy as jnp
from jax import lax
from jax.experimental import pallas as pl
from jax.experimental.pallas import tpu as pltpu
from jax.sharding import PartitionSpec as P

CH = 12
L = 300
BLK = 128
EPS = 1e-06
CAP = 4
UNIT = 32
SHIFTS = 16
GROUP = 16
VMEM_LIMIT = 60 * 1024 * 1024
NT = (((1,), (1,)), ((), ()))
TN = (((0,), (0,)), ((), ()))


def lanes_of(shape):
    return lax.broadcasted_iota(jnp.int32, shape, len(shape) - 1)


def rows_of(shape):
    return lax.broadcasted_iota(jnp.int32, shape, len(shape) - 2)


def to_bf16(values):
    return values.astype(jnp.bfloat16)


def to_f32(values):
    return values.astype(jnp.float32)


def pack_kernel(station_ref, block_ref, templates_ref, sent_ref, place_ref, padded, units, units16, used):
    templates = templates_ref.shape[0]
    rows_part = station_ref.shape[1]
    padded[...] = jnp.zeros_like(padded)
    units[...] = jnp.zeros_like(units)
    for k in range(templates):
        values = to_f32(templates_ref[k])
        centred = values - jnp.sum(values, axis=1, keepdims=True) / L
        power = jnp.sum(centred * centred, axis=1, keepdims=True) / L
        factor = 1.0 / (60.0 * jnp.sqrt(power + EPS))
        padded[k, :, 0:L] = to_f32(to_bf16(centred))
        units[k, 0:12, :] = padded[k, :, 0:128]
        units[k, 12:24, :] = padded[k, :, 128:256]
        rest = padded[k, :, 256:384]
        units[k, 24:30, :] = rest[0:6] + pltpu.roll(rest, 64, 1)[6:12]
        high = to_f32(to_bf16(factor))
        middle = to_f32(to_bf16(factor - high))
        low = to_f32(to_bf16(factor - high - middle))
        lane, row = lanes_of((CH, 128)), rows_of((CH, 128))
        spread = jnp.where(
            lane == row,
            high,
            jnp.where(lane == row + 16, middle, jnp.where(lane == row + 32, low, 0.0)),
        )
        units[k, 30:31, :] = jnp.sum(spread, axis=0, keepdims=True)
        units16[k] = to_bf16(units[k])

    def clear(h, carry):
        sent_ref[pl.ds(CAP * h, CAP)] = jnp.zeros((CAP, UNIT, 128), jnp.bfloat16)
        used[h] = 0
        return carry

    lax.fori_loop(0, used.shape[0], clear, 0)
    lane, row = lanes_of((16, 128)), rows_of((16, 128))
    at_station = (row == 14) & (lane == 48)
    at_block = (row == 14) & (lane == 49)

    def place(r, carry):
        k = r // rows_part
        station = station_ref[k, r % rows_part]
        block = block_ref[k, r % rows_part] & 31
        holder = station // 8
        rank = jnp.minimum(used[holder], CAP - 1)
        used[holder] = rank + 1
        slot = holder * CAP + rank
        place_ref[r] = slot
        sent_ref[slot, 0:16, :] = units16[k, 0:16, :]
        upper = units[k, 16:32, :]
        upper = jnp.where(at_station, (station & 7).astype(jnp.float32), upper)
        upper = jnp.where(at_block, block.astype(jnp.float32), upper)
        sent_ref[slot, 16:32, :] = to_bf16(upper)
        return carry

    lax.fori_loop(0, templates * rows_part, place, 0, unroll=4)


def pack(station, block, templates, holders):
    count = templates.shape[0]
    return pl.pallas_call(
        pack_kernel,
        out_shape=(
            jax.ShapeDtypeStruct((holders * CAP, UNIT, 128), jnp.bfloat16),
            jax.ShapeDtypeStruct((count * station.shape[1],), jnp.int32),
        ),
        in_specs=[
            pl.BlockSpec(memory_space=pltpu.SMEM),
            pl.BlockSpec(memory_space=pltpu.SMEM),
            pl.BlockSpec(memory_space=pltpu.VMEM),
        ],
        out_specs=(
            pl.BlockSpec(memory_space=pltpu.VMEM),
            pl.BlockSpec(memory_space=pltpu.SMEM),
        ),
        scratch_shapes=[
            pltpu.VMEM((count, CH, 384), jnp.float32),
            pltpu.VMEM((count, UNIT, 128), jnp.float32),
            pltpu.VMEM((count, UNIT, 128), jnp.bfloat16),
            pltpu.SMEM((holders,), jnp.int32),
        ],
        compiler_params=pltpu.CompilerParams(vmem_limit_bytes=VMEM_LIMIT),
    )(station, block, templates)


def station_kernel(wave_ref, tail_ref, shifted_ref, inverse_ref, signal, stacked):
    segment = wave_ref.shape[2]
    blocks = inverse_ref.shape[1]
    pieces = shifted_ref.shape[1]
    signal[CH:16, :] = jnp.zeros_like(signal[CH:16, :])
    signal[0:CH, 0:segment] = to_f32(wave_ref[0])
    signal[0:CH, segment:] = to_f32(tail_ref[0])
    lane, row = lanes_of((SHIFTS, 128)), rows_of((SHIFTS, 128))
    source = (lane + 8 * row) & 127
    inside = lane + 8 * row < 128

    def shift(piece, carry):
        start = pl.multiple_of(piece * 128, 128)
        here = signal[:, pl.ds(start, 128)]
        after = signal[:, pl.ds(start + 128, 128)]
        for c in range(CH):
            left = jnp.take_along_axis(jnp.broadcast_to(here[c : c + 1], (SHIFTS, 128)), source, axis=1)
            right = jnp.take_along_axis(jnp.broadcast_to(after[c : c + 1], (SHIFTS, 128)), source, axis=1)
            shifted_ref[0, piece, c] = to_bf16(jnp.where(inside, left, right))
        return carry

    lax.fori_loop(0, pieces, shift, 0)
    for b in range(blocks):
        stacked[16 * b : 16 * b + 16, :] = signal[:, 128 * b : 128 * b + 512]
    sample, position = rows_of((512, 128)), lanes_of((512, 128))
    band = to_bf16(jnp.where((sample >= position) & (sample < position + L), 1.0, 0.0))
    values = stacked[...]
    squares = values * values
    high = to_bf16(squares)
    low = to_bf16(squares - to_f32(high))
    first = jnp.dot(to_bf16(values), band, preferred_element_type=jnp.float32) / L
    second = (
        jnp.dot(high, band, preferred_element_type=jnp.float32)
        + jnp.dot(low, band, preferred_element_type=jnp.float32)
    ) / L
    inverse = 1.0 / jnp.sqrt(second - first * first + EPS)
    inverse_ref[0] = inverse.reshape(blocks, 16, 128)


def station_tables(wave, tail):
    stations, channels, segment = wave.shape
    blocks = segment // BLK
    extra = tail.shape[2]
    return pl.pallas_call(
        station_kernel,
        grid=(stations,),
        out_shape=(
            jax.ShapeDtypeStruct((stations, blocks + 2, channels, SHIFTS, 128), jnp.bfloat16),
            jax.ShapeDtypeStruct((stations, blocks, 16, 128), jnp.float32),
        ),
        in_specs=[
            pl.BlockSpec((1, channels, segment), lambda s: (s, 0, 0)),
            pl.BlockSpec((1, channels, extra), lambda s: (s, 0, 0)),
        ],
        out_specs=(
            pl.BlockSpec((1, blocks + 2, channels, SHIFTS, 128), lambda s: (s, 0, 0, 0, 0)),
            pl.BlockSpec((1, blocks, 16, 128), lambda s: (s, 0, 0, 0)),
        ),
        scratch_shapes=[
            pltpu.VMEM((16, segment + extra), jnp.float32),
            pltpu.VMEM((16 * blocks, 512), jnp.float32),
        ],
        compiler_params=pltpu.CompilerParams(vmem_limit_bytes=32 * 1024 * 1024),
        cost_estimate=pl.CostEstimate(flops=3_000_000_000, bytes_accessed=20_000_000, transcendentals=500_000),
    )(wave, tail)


def score_kernel(
    station_ref, block_ref, units_ref, marks_ref, shifted_ref, inverse_ref, scores_ref, kernels, windows
):
    lane, row = lanes_of((8, 128)), rows_of((8, 128))
    before = lane < row
    low_half = lane < 64
    member = lane // SHIFTS
    inverse_source = 8 * (lane % SHIFTS) + row
    natural_source = SHIFTS * row + lane // 8
    expand = to_bf16(jnp.where(lanes_of((GROUP, 256)) // SHIFTS == rows_of((GROUP, 256)), 1.0, 0.0))

    def template_rows(unit):
        swapped = pltpu.roll(unit, 64, 1)
        result = []
        for c in range(CH):
            third = unit[24 + c : 25 + c] if c < 6 else swapped[18 + c : 19 + c]
            parts = [unit[c : c + 1], unit[12 + c : 13 + c], third]
            parts = [jnp.broadcast_to(part, (8, 128)) for part in parts]
            parts[2] = jnp.where(low_half, parts[2], 0.0)
            turned = [pltpu.roll(part, 0, 1, stride=1, stride_axis=0) for part in parts]
            result.append(
                [
                    jnp.where(before, 0.0, turned[0]),
                    jnp.where(before, turned[0], turned[1]),
                    jnp.where(before, turned[1], turned[2]),
                ]
            )
        return result

    def one_group(group, carry):
        base = group * GROUP
        for pair in range(GROUP // 2):
            rows = []
            for g in (2 * pair, 2 * pair + 1):
                station, block = station_ref[base + g], block_ref[base + g]
                for a in range(3):
                    windows[:, 16 * g : 16 * g + 16, 128 * a : 128 * a + 128] = shifted_ref[station, block + a]
                rows.append(template_rows(to_f32(units_ref[base + g])))
            for c in range(CH):
                for a in range(3):
                    both = jnp.concatenate([rows[0][c][a], rows[1][c][a]], axis=0)
                    kernels[c, 16 * pair : 16 * pair + 16, 128 * a : 128 * a + 128] = to_bf16(both)
        marks = marks_ref[pl.ds(pl.multiple_of(base, GROUP), GROUP), :]
        spread = lax.dot_general(marks, expand, TN, preferred_element_type=jnp.float32)
        factors = spread[0:12] + spread[16:28] + spread[32:44]
        totals = [jnp.zeros((8, 128), jnp.float32) for _ in range(2)]
        for c in range(CH):
            products = lax.dot_general(kernels[c], windows[c], NT, preferred_element_type=jnp.float32)
            for half in range(2):
                chosen = jnp.zeros((8, 128), jnp.float32)
                scale = jnp.zeros((8, 128), jnp.float32)
                for m in range(8):
                    g = 8 * half + m
                    station, block = station_ref[base + g], block_ref[base + g]
                    inverse = jnp.broadcast_to(inverse_ref[station, block, c : c + 1, :], (8, 128))
                    inverse = jnp.take_along_axis(inverse, inverse_source, axis=1)
                    mine = products[8 * g : 8 * g + 8, 128 * half : 128 * half + 128]
                    chosen = jnp.where(member == m, mine, chosen)
                    scale = jnp.where(member == m, inverse, scale)
                factor = factors[c : c + 1, 128 * half : 128 * half + 128]
                totals[half] = totals[half] + chosen * scale * factor
        for half in range(2):
            natural = jnp.zeros((8, 128), jnp.float32)
            for i in range(8):
                spread_row = jnp.broadcast_to(totals[half][i : i + 1], (8, 128))
                spread_row = jnp.take_along_axis(spread_row, natural_source, axis=1)
                natural = jnp.where(lane % 8 == i, spread_row, natural)
            for o in range(2):
                scores_ref[group * 4 + half * 2 + o] = natural[4 * o : 4 * o + 4]
        return carry

    lax.fori_loop(0, units_ref.shape[0] // GROUP, one_group, 0)


def slot_scores(stations, blocks, units, marks, shifted, inverse):
    slots = units.shape[0]
    smem = pl.BlockSpec(memory_space=pltpu.SMEM)
    vmem = pl.BlockSpec(memory_space=pltpu.VMEM)
    return pl.pallas_call(
        score_kernel,
        out_shape=jax.ShapeDtypeStruct((slots // CAP, CAP, BLK), jnp.float32),
        in_specs=[smem, smem, vmem, vmem, vmem, vmem],
        out_specs=vmem,
        scratch_shapes=[
            pltpu.VMEM((CH, 8 * GROUP, 384), jnp.bfloat16),
            pltpu.VMEM((CH, SHIFTS * GROUP, 384), jnp.bfloat16),
        ],
        compiler_params=pltpu.CompilerParams(vmem_limit_bytes=VMEM_LIMIT),
    )(stations, blocks, units, marks, shifted, inverse)


def unpack_kernel(place_ref, limit_ref, scores_ref, out_ref):
    templates, rows_part, _ = out_ref.shape
    for k in range(templates):
        for r in range(rows_part):
            slot = place_ref[k * rows_part + r]
            found = scores_ref[slot // CAP, pl.ds(slot % CAP, 1), :]
            out_ref[k, r : r + 1, :] = jnp.where(r < limit_ref[k], found, 0.0)


def unpack(place, limit, scores, shape):
    smem = pl.BlockSpec(memory_space=pltpu.SMEM)
    vmem = pl.BlockSpec(memory_space=pltpu.VMEM)
    return pl.pallas_call(
        unpack_kernel,
        out_shape=jax.ShapeDtypeStruct(shape, jnp.float32),
        in_specs=[smem, smem, vmem],
        out_specs=vmem,
        compiler_params=pltpu.CompilerParams(vmem_limit_bytes=VMEM_LIMIT),
    )(place, limit, scores)


def local(waveforms, templates, det_station, det_block, det_count):
    own_count, rows_part = det_station.shape
    wide_count = lax.axis_size("wide")
    narrow_count = lax.axis_size("narrow")
    exchange = functools.partial(lax.all_to_all, axis_name="wide", split_axis=0, concat_axis=0, tiled=True)
    sent, place = pack(det_station, det_block, templates, wide_count)
    units = exchange(sent.reshape(wide_count, CAP * UNIT, 128)).reshape(wide_count * CAP, UNIT, 128)
    tail = lax.ppermute(
        waveforms[:, :, : 3 * BLK], "narrow", [(i, i - 1) for i in range(1, narrow_count)]
    )
    shifted, inverse = station_tables(waveforms, tail)
    marks = units[:, 30, :]
    scores = slot_scores(
        marks[:, 48].astype(jnp.int32), marks[:, 49].astype(jnp.int32), units, marks, shifted, inverse
    )
    returned = exchange(scores)
    limit = det_count - lax.axis_index("narrow") * rows_part
    return unpack(place, limit, returned, (own_count, rows_part, BLK))


def solution(mesh):
    placed = (
        P("wide", None, "narrow"),
        P("wide", None, None),
        P("wide", "narrow"),
        P("wide", "narrow"),
        P("wide"),
    )
    return jax.shard_map(
        local, mesh=mesh, in_specs=placed, out_specs=P("wide", "narrow", None), check_vma=False
    )
```

```python
import jax
import jax.numpy as jnp
from jax import lax
from jax.experimental import pallas as pl
from jax.experimental.pallas import tpu as pltpu
from jax.sharding import PartitionSpec as P

CH = 12
L = 300
BLK = 128
EPS = 1e-06
CAP = 4
UNIT = 32
PLANE = 8
X, Y = 4, 2
PLANE_STEPS = ((0, 0), (1, 0), (3, 0), (0, 1), (2, 0), (1, 1), (3, 1), (2, 1))
Z_STEPS = (0, 1, 7, 2, 6, 3, 5, 4)
SHIFTS = 16
GROUP = 16
VMEM_LIMIT = 24 * 1024 * 1024
NT = (((1,), (1,)), ((), ()))
TN = (((0,), (0,)), ((), ()))


def lanes_of(shape):
    return lax.broadcasted_iota(jnp.int32, shape, len(shape) - 1)


def rows_of(shape):
    return lax.broadcasted_iota(jnp.int32, shape, len(shape) - 2)


def to_bf16(values):
    return values.astype(jnp.bfloat16)


def to_f32(values):
    return values.astype(jnp.float32)


def read_scalars(rows, weights, staged, scalars, sem):
    lane = lanes_of((8, 128))
    picked = jnp.zeros((8, 128), jnp.float32)
    for place, weight in weights:
        picked = jnp.where(lane == place, float(weight), picked)
    values = lax.dot_general(to_bf16(picked), rows, NT, preferred_element_type=jnp.float32)
    staged[...] = values.astype(jnp.int32)
    copy = pltpu.make_async_copy(staged, scalars, sem)
    copy.start()
    copy.wait()


def pack_kernel(station_ref, block_ref, templates_ref, *refs):
    sent_refs, (place_ref, padded, units, table, used) = refs[: len(Z_STEPS)], refs[len(Z_STEPS) :]
    channels, templates, _ = templates_ref.shape
    rows_part = station_ref.shape[1]
    values = to_f32(templates_ref[...])
    centred = values - jnp.sum(values, axis=2, keepdims=True) / L
    power = jnp.sum(centred * centred, axis=2, keepdims=True) / L
    factor = 1.0 / (60.0 * jnp.sqrt(power + EPS))
    padded[...] = jnp.zeros_like(padded)
    padded[:, :, 0:L] = to_f32(to_bf16(centred))
    high = to_f32(to_bf16(factor))
    middle = to_f32(to_bf16(factor - high))
    low = to_f32(to_bf16(factor - high - middle))
    lane = lanes_of((templates, 128))
    marks = jnp.zeros((templates, 128), jnp.float32)
    for c in range(channels):
        marks = jnp.where(lane == c, high[c], marks)
        marks = jnp.where(lane == c + 16, middle[c], marks)
        marks = jnp.where(lane == c + 32, low[c], marks)
        units[:, c, :] = padded[c, :, 0:128]
        units[:, 12 + c, :] = padded[c, :, 128:256]
    for c in range(6):
        units[:, 24 + c, :] = padded[c, :, 256:384] + pltpu.roll(padded[c + 6, :, 256:384], 64, 1)
    units[:, 30, :] = marks
    units[:, 31, :] = jnp.zeros_like(marks)
    for sent_ref in sent_refs:
        sent_ref[0:templates] = to_bf16(units[...])
    table[...] = jnp.zeros_like(table)

    def clear(h, carry):
        used[h] = 0
        return carry

    lax.fori_loop(0, used.shape[0], clear, 0, unroll=8)
    lane = lanes_of((1, 128))

    def place(r, carry):
        k = r // rows_part
        station = station_ref[k, r % rows_part]
        block = block_ref[k, r % rows_part] & 31
        holder = station // 8
        rank = jnp.minimum(used[holder], CAP - 1)
        used[holder] = rank + 1
        slot = holder * CAP + rank
        place_ref[r] = slot
        entry = jnp.where(lane == 0, k, jnp.where(lane == 48, station & 7, jnp.where(lane == 49, block, 0)))
        table[pl.ds(slot, 1), :] = to_f32(entry)
        return carry

    lax.fori_loop(0, templates * rows_part, place, 0, unroll=8)
    here = lax.axis_index("wide") // PLANE
    for step, sent_ref in zip(Z_STEPS, sent_refs):
        start = pl.multiple_of((here + step) % len(Z_STEPS) * UNIT, UNIT)
        sent_ref[templates] = to_bf16(table[pl.ds(start, UNIT), :])


def pack(station, block, templates, holders):
    channels, count, _ = templates.shape
    smem = pl.BlockSpec(memory_space=pltpu.SMEM)
    vmem = pl.BlockSpec(memory_space=pltpu.VMEM)
    return pl.pallas_call(
        pack_kernel,
        out_shape=(
            *[jax.ShapeDtypeStruct((count + 1, UNIT, 128), jnp.bfloat16)] * len(Z_STEPS),
            jax.ShapeDtypeStruct((count * station.shape[1],), jnp.int32),
        ),
        in_specs=[smem, smem, vmem],
        out_specs=(*[vmem] * len(Z_STEPS), smem),
        scratch_shapes=[
            pltpu.VMEM((channels, count, 384), jnp.float32),
            pltpu.VMEM((count, UNIT, 128), jnp.float32),
            pltpu.VMEM((holders * CAP, 128), jnp.float32),
            pltpu.SMEM((holders,), jnp.int32),
        ],
        compiler_params=pltpu.CompilerParams(vmem_limit_bytes=VMEM_LIMIT),
    )(station, block, templates)


def member_after(member, step):
    return (member // Y + step[0]) % X * Y + (member % Y + step[1]) % Y


def route_kernel(*refs):
    sources = len(Z_STEPS)
    held_refs, sent_refs = refs[:sources], refs[sources : sources + PLANE]
    tables, staged, chosen_ref, sem = refs[sources + PLANE :]
    me = lax.axis_index("wide") % PLANE
    last = held_refs[0].shape[0] - 1
    for source, held_ref in enumerate(held_refs):
        tables[source] = to_f32(held_ref[last])
    entries = jnp.concatenate([held_ref[last] for held_ref in held_refs], axis=0)
    read_scalars(entries, ((0, 1),), staged, chosen_ref, sem)
    lane, row = lanes_of((16, 128)), rows_of((16, 128))
    marked = (row == 14) & (lane >= 48) & (lane < 50)
    for step, sent_ref in zip(PLANE_STEPS, sent_refs):
        first = member_after(me, step) * CAP
        for source, held_ref in enumerate(held_refs):
            for j in range(CAP):
                chosen = chosen_ref[0, source * UNIT + first + j]
                slot = source * CAP + j
                sent_ref[slot, 0:16, :] = held_ref[chosen, 0:16, :]
                upper = to_f32(held_ref[chosen, 16:32, :])
                entry = jnp.broadcast_to(tables[source, pl.ds(first + j, 1), :], (16, 128))
                sent_ref[slot, 16:32, :] = to_bf16(jnp.where(marked, entry, upper))


def route(held):
    sources = len(held)
    vmem = pl.BlockSpec(memory_space=pltpu.VMEM)
    return pl.pallas_call(
        route_kernel,
        out_shape=[jax.ShapeDtypeStruct((sources * CAP, UNIT, 128), jnp.bfloat16)] * PLANE,
        in_specs=[vmem] * sources,
        out_specs=[vmem] * PLANE,
        scratch_shapes=[
            pltpu.VMEM((sources, UNIT, 128), jnp.float32),
            pltpu.VMEM((8, sources * UNIT), jnp.int32),
            pltpu.SMEM((8, sources * UNIT), jnp.int32),
            pltpu.SemaphoreType.DMA,
        ],
        compiler_params=pltpu.CompilerParams(vmem_limit_bytes=VMEM_LIMIT),
    )(*held)


def station_kernel(wave_ref, tail_ref, shifted_ref, inverse_ref, signal, stacked):
    segment = wave_ref.shape[2]
    blocks = inverse_ref.shape[1]
    pieces = shifted_ref.shape[1]
    signal[CH:16, :] = jnp.zeros_like(signal[CH:16, :])
    signal[0:CH, 0:segment] = to_f32(wave_ref[0])
    signal[0:CH, segment:] = to_f32(tail_ref[0])
    lane, row = lanes_of((SHIFTS, 128)), rows_of((SHIFTS, 128))
    source = (lane + 8 * row) & 127
    inside = lane + 8 * row < 128

    for c in range(CH):
        before = None
        for piece in range(pieces + 1):
            here = jnp.broadcast_to(signal[c : c + 1, 128 * piece : 128 * piece + 128], (SHIFTS, 128))
            here = jnp.take_along_axis(here, source, axis=1)
            if piece > 0:
                shifted_ref[0, piece - 1, c] = to_bf16(jnp.where(inside, before, here))
            before = here
    for b in range(blocks):
        stacked[16 * b : 16 * b + 16, :] = signal[:, 128 * b : 128 * b + 512]
    sample, position = rows_of((512, 128)), lanes_of((512, 128))
    band = to_bf16(jnp.where((sample >= position) & (sample < position + L), 1.0, 0.0))
    values = stacked[...]
    squares = values * values
    high = to_bf16(squares)
    low = to_bf16(squares - to_f32(high))
    first = jnp.dot(to_bf16(values), band, preferred_element_type=jnp.float32) / L
    second = (
        jnp.dot(high, band, preferred_element_type=jnp.float32)
        + jnp.dot(low, band, preferred_element_type=jnp.float32)
    ) / L
    inverse = 1.0 / jnp.sqrt(second - first * first + EPS)
    inverse_ref[0] = inverse.reshape(blocks, 16, 128)


def station_tables(wave, tail):
    stations, channels, segment = wave.shape
    blocks = segment // BLK
    extra = tail.shape[2]
    return pl.pallas_call(
        station_kernel,
        grid=(stations,),
        out_shape=(
            jax.ShapeDtypeStruct((stations, blocks + 2, channels, SHIFTS, 128), jnp.bfloat16),
            jax.ShapeDtypeStruct((stations, blocks, 16, 128), jnp.float32),
        ),
        in_specs=[
            pl.BlockSpec((1, channels, segment), lambda s: (s, 0, 0)),
            pl.BlockSpec((1, channels, extra), lambda s: (s, 0, 0)),
        ],
        out_specs=(
            pl.BlockSpec((1, blocks + 2, channels, SHIFTS, 128), lambda s: (s, 0, 0, 0, 0)),
            pl.BlockSpec((1, blocks, 16, 128), lambda s: (s, 0, 0, 0)),
        ),
        scratch_shapes=[
            pltpu.VMEM((16, segment + extra), jnp.float32),
            pltpu.VMEM((16 * blocks, 512), jnp.float32),
        ],
        compiler_params=pltpu.CompilerParams(vmem_limit_bytes=VMEM_LIMIT),
        cost_estimate=pl.CostEstimate(flops=3_000_000_000, bytes_accessed=20_000_000, transcendentals=500_000),
    )(wave, tail)


def score_kernel(
    first_ref, second_ref, shifted_ref, inverse_ref, scores_ref, rows, marked, staged, codes, sem
):
    lane, row = lanes_of((8, 128)), rows_of((8, 128))
    before = lane < row
    member = lane // SHIFTS
    inverse_source = 8 * (lane % SHIFTS) + row
    natural_source = SHIFTS * row + lane // 8
    expand = to_bf16(jnp.where(lanes_of((GROUP, 256)) // SHIFTS == rows_of((GROUP, 256)), 1.0, 0.0))
    count = first_ref.shape[0]
    for start, units_ref in ((0, first_ref), (count, second_ref)):
        units = units_ref[...]
        marked[start : start + count] = units[:, 30, :]
        third = to_f32(units[:, 16:32, :])[:, 8:16, :]
        low_half = lanes_of(third.shape) < 64
        rows[start : start + count, 0:24, :] = to_f32(units)[:, 0:24, :]
        rows[start : start + count, 24:32, :] = jnp.where(low_half, third, 0.0)
        rows[start : start + count, 32:40, :] = jnp.where(low_half, pltpu.roll(third, 64, 2), 0.0)
    read_scalars(marked[...], ((48, 32), (49, 1)), staged, codes, sem)

    def template_rows(g, c):
        turned = []
        for r in (c, 12 + c, 24 + c if c < 6 else 26 + c):
            part = jnp.broadcast_to(rows[g, r : r + 1, :], (8, 128))
            turned.append(pltpu.roll(part, 0, 1, stride=1, stride_axis=0))
        return [
            jnp.where(before, 0.0, turned[0]),
            jnp.where(before, turned[0], turned[1]),
            jnp.where(before, turned[1], turned[2]),
        ]

    def score(group, carry):
        base = pl.multiple_of(group * GROUP, GROUP)
        marks = marked[pl.ds(base, GROUP), :]
        spread = lax.dot_general(marks, expand, TN, preferred_element_type=jnp.float32)
        factors = spread[0:12] + spread[16:28] + spread[32:44]
        totals = [jnp.zeros((8, 128), jnp.float32) for _ in range(2)]
        places = [(codes[0, base + g] // 32, codes[0, base + g] % 32) for g in range(GROUP)]
        for c in range(CH):
            pairs = []
            for pair in range(GROUP // 2):
                one, two = template_rows(base + 2 * pair, c), template_rows(base + 2 * pair + 1, c)
                both = [to_bf16(jnp.concatenate([one[a], two[a]], axis=0)) for a in range(3)]
                pairs.append(jnp.concatenate(both, axis=1))
            products = lax.dot_general(
                jnp.concatenate(pairs, axis=0),
                jnp.concatenate(
                    [
                        jnp.concatenate([shifted_ref[s, b + a, c] for s, b in places], axis=0)
                        for a in range(3)
                    ],
                    axis=1,
                ),
                NT,
                preferred_element_type=jnp.float32,
            )
            for half in range(2):
                chosen = jnp.zeros((8, 128), jnp.float32)
                scale = jnp.zeros((8, 128), jnp.float32)
                for m in range(8):
                    g = 8 * half + m
                    station, block = places[g]
                    inverse = jnp.broadcast_to(inverse_ref[station, block, c : c + 1, :], (8, 128))
                    inverse = jnp.take_along_axis(inverse, inverse_source, axis=1)
                    mine = products[8 * g : 8 * g + 8, 128 * half : 128 * half + 128]
                    chosen = jnp.where(member == m, mine, chosen)
                    scale = jnp.where(member == m, inverse, scale)
                factor = factors[c : c + 1, 128 * half : 128 * half + 128]
                totals[half] = totals[half] + chosen * scale * factor
        for half in range(2):
            natural = jnp.zeros((8, 128), jnp.float32)
            for i in range(8):
                spread_row = jnp.broadcast_to(totals[half][i : i + 1], (8, 128))
                spread_row = jnp.take_along_axis(spread_row, natural_source, axis=1)
                natural = jnp.where(lane % 8 == i, spread_row, natural)
            for o in range(2):
                scores_ref[group * 4 + half * 2 + o] = natural[4 * o : 4 * o + 4]
        return carry

    lax.fori_loop(0, 2 * count // GROUP, score, 0)


def slot_scores(first, second, shifted, inverse):
    slots = 2 * first.shape[0]
    vmem = pl.BlockSpec(memory_space=pltpu.VMEM)
    return pl.pallas_call(
        score_kernel,
        out_shape=jax.ShapeDtypeStruct((slots // CAP, CAP, BLK), jnp.float32),
        in_specs=[vmem] * 4,
        out_specs=vmem,
        scratch_shapes=[
            pltpu.VMEM((slots, 40, 128), jnp.float32),
            pltpu.VMEM((slots, 128), jnp.bfloat16),
            pltpu.VMEM((8, slots), jnp.int32),
            pltpu.SMEM((8, slots), jnp.int32),
            pltpu.SemaphoreType.DMA,
        ],
        compiler_params=pltpu.CompilerParams(vmem_limit_bytes=VMEM_LIMIT),
        cost_estimate=pl.CostEstimate(flops=4_000_000_000, bytes_accessed=4_000_000, transcendentals=0),
    )(first, second, shifted, inverse)


def arrange_kernel(*refs):
    scores_refs, out_ref = refs[:-1], refs[-1]
    z, me = lax.axis_index("wide") // PLANE, lax.axis_index("wide") % PLANE
    for number, step in enumerate(PLANE_STEPS):
        scores_ref, start = scores_refs[number // 2], number % 2 * len(Z_STEPS)
        member = member_after(me, (X - step[0], Y - step[1]))
        for source, offset in enumerate(Z_STEPS):
            owner = (z + len(Z_STEPS) - offset) % len(Z_STEPS) * PLANE + member
            out_ref[owner] = scores_ref[start + source]


def arrange(scores):
    vmem = pl.BlockSpec(memory_space=pltpu.VMEM)
    return pl.pallas_call(
        arrange_kernel,
        out_shape=jax.ShapeDtypeStruct((len(Z_STEPS) * PLANE, CAP, BLK), jnp.float32),
        in_specs=[vmem] * len(scores),
        out_specs=vmem,
        compiler_params=pltpu.CompilerParams(vmem_limit_bytes=VMEM_LIMIT),
    )(*scores)


def unpack_kernel(place_ref, limit_ref, scores_ref, out_ref):
    templates, rows_part, _ = out_ref.shape
    for k in range(templates):
        for r in range(rows_part):
            slot = place_ref[k * rows_part + r]
            found = scores_ref[slot // CAP, pl.ds(slot % CAP, 1), :]
            out_ref[k, r : r + 1, :] = jnp.where(r < limit_ref[k], found, 0.0)


def unpack(place, limit, scores, shape):
    smem = pl.BlockSpec(memory_space=pltpu.SMEM)
    vmem = pl.BlockSpec(memory_space=pltpu.VMEM)
    return pl.pallas_call(
        unpack_kernel,
        out_shape=jax.ShapeDtypeStruct(shape, jnp.float32),
        in_specs=[smem, smem, vmem],
        out_specs=vmem,
        compiler_params=pltpu.CompilerParams(vmem_limit_bytes=VMEM_LIMIT),
    )(place, limit, scores)


def local(waveforms, templates, det_station, det_block, det_count):
    own_count, rows_part = det_station.shape
    wide_count = lax.axis_size("wide")
    narrow_count = lax.axis_size("narrow")
    planes = wide_count // PLANE
    members = [(z, p) for z in range(planes) for p in range(PLANE)]
    *sent, place = pack(det_station, det_block, jnp.transpose(templates, (1, 0, 2)), wide_count)
    held = [sent[0]]
    for step, value in zip(Z_STEPS[1:], sent[1:]):
        pairs = [(PLANE * z + p, PLANE * ((z + step) % planes) + p) for z, p in members]
        held.append(lax.ppermute(value, "wide", pairs))
    tail = lax.ppermute(
        waveforms[:, :, : 3 * BLK], "narrow", [(i, i - 1) for i in range(1, narrow_count)]
    )
    shifted, inverse = station_tables(waveforms, tail)
    routed = route(held)
    arrived = []
    for step, units in zip(PLANE_STEPS, routed):
        if step != (0, 0):
            pairs = [(PLANE * z + p, PLANE * z + member_after(p, step)) for z, p in members]
            units = lax.ppermute(units, "wide", pairs)
        arrived.append(units)
    scores = [slot_scores(*arrived[i : i + 2], shifted, inverse) for i in range(0, PLANE, 2)]
    returned = lax.all_to_all(arrange(scores), "wide", split_axis=0, concat_axis=0, tiled=True)
    limit = det_count - lax.axis_index("narrow") * rows_part
    return unpack(place, limit, returned, (own_count, rows_part, BLK))


def solution(mesh):
    placed = (
        P("wide", None, "narrow"),
        P("wide", None, None),
        P("wide", "narrow"),
        P("wide", "narrow"),
        P("wide"),
    )
    return jax.shard_map(
        local, mesh=mesh, in_specs=placed, out_specs=P("wide", "narrow", None), check_vma=False
    )
```

```python
import jax
import jax.numpy as jnp
from jax import lax
from jax.experimental import pallas as pl
from jax.experimental.pallas import tpu as pltpu
from jax.sharding import PartitionSpec as P

CH = 12
L = 300
BLK = 128
EPS = 1e-06
CAP = 4
UNIT = 32
PLANE = 8
X, Y = 4, 2
PLANE_STEPS = ((0, 0), (1, 0), (3, 0), (0, 1), (2, 0), (1, 1), (3, 1), (2, 1))
CALLS = ((1, 2), (3, 4), (5, 6), (0, 7))
SHIFTS = 16
GROUP = 16
VMEM_LIMIT = 24 * 1024 * 1024
NT = (((1,), (1,)), ((), ()))
TN = (((0,), (0,)), ((), ()))


def lanes_of(shape):
    return lax.broadcasted_iota(jnp.int32, shape, len(shape) - 1)


def rows_of(shape):
    return lax.broadcasted_iota(jnp.int32, shape, len(shape) - 2)


def to_bf16(values):
    return values.astype(jnp.bfloat16)


def to_f32(values):
    return values.astype(jnp.float32)


def read_scalars(rows, weights, staged, scalars, sem):
    lane = lanes_of((8, 128))
    picked = jnp.zeros((8, 128), jnp.float32)
    for place, weight in weights:
        picked = jnp.where(lane == place, float(weight), picked)
    values = lax.dot_general(to_bf16(picked), rows, NT, preferred_element_type=jnp.float32)
    staged[...] = values.astype(jnp.int32)
    copy = pltpu.make_async_copy(staged, scalars, sem)
    copy.start()
    return copy


def pack_kernel(station_ref, block_ref, templates_ref, sent_ref, place_ref, padded, units, table, used):
    channels, templates, _ = templates_ref.shape
    rows_part = station_ref.shape[1]
    values = to_f32(templates_ref[...])
    centred = values - jnp.sum(values, axis=2, keepdims=True) / L
    power = jnp.sum(centred * centred, axis=2, keepdims=True) / L
    factor = 1.0 / (60.0 * jnp.sqrt(power + EPS))
    padded[...] = jnp.zeros_like(padded)
    padded[:, :, 0:L] = to_f32(to_bf16(centred))
    high = to_f32(to_bf16(factor))
    middle = to_f32(to_bf16(factor - high))
    low = to_f32(to_bf16(factor - high - middle))
    lane = lanes_of((templates, 128))
    marks = jnp.zeros((templates, 128), jnp.float32)
    for c in range(channels):
        marks = jnp.where(lane == c, high[c], marks)
        marks = jnp.where(lane == c + 16, middle[c], marks)
        marks = jnp.where(lane == c + 32, low[c], marks)
        units[:, c, :] = padded[c, :, 0:128]
        units[:, 12 + c, :] = padded[c, :, 128:256]
    for c in range(6):
        units[:, 24 + c, :] = padded[c, :, 256:384] + pltpu.roll(padded[c + 6, :, 256:384], 64, 1)
    units[:, 30, :] = marks
    units[:, 31, :] = jnp.zeros_like(marks)
    for z in range(sent_ref.shape[0]):
        sent_ref[z, 0:templates] = to_bf16(units[...])
    table[...] = jnp.zeros_like(table)

    def clear(h, carry):
        used[h] = 0
        return carry

    lax.fori_loop(0, used.shape[0], clear, 0, unroll=8)
    lane = lanes_of((1, 128))

    def place(r, carry):
        k = r // rows_part
        station = station_ref[k, r % rows_part]
        block = block_ref[k, r % rows_part] & 31
        holder = station // 8
        rank = jnp.minimum(used[holder], CAP - 1)
        used[holder] = rank + 1
        slot = holder * CAP + rank
        place_ref[r] = slot
        entry = jnp.where(lane == 0, k, jnp.where(lane == 48, station & 7, jnp.where(lane == 49, block, 0)))
        table[pl.ds(slot, 1), :] = to_f32(entry)
        return carry

    lax.fori_loop(0, templates * rows_part, place, 0, unroll=8)
    for z in range(sent_ref.shape[0]):
        sent_ref[z, templates] = to_bf16(table[UNIT * z : UNIT * z + UNIT, :])


def pack(station, block, templates, holders):
    channels, count, _ = templates.shape
    smem = pl.BlockSpec(memory_space=pltpu.SMEM)
    vmem = pl.BlockSpec(memory_space=pltpu.VMEM)
    return pl.pallas_call(
        pack_kernel,
        out_shape=(
            jax.ShapeDtypeStruct((holders // PLANE, count + 1, UNIT, 128), jnp.bfloat16),
            jax.ShapeDtypeStruct((count * station.shape[1],), jnp.int32),
        ),
        in_specs=[smem, smem, vmem],
        out_specs=(vmem, smem),
        scratch_shapes=[
            pltpu.VMEM((channels, count, 384), jnp.float32),
            pltpu.VMEM((count, UNIT, 128), jnp.float32),
            pltpu.VMEM((holders * CAP, 128), jnp.float32),
            pltpu.SMEM((holders,), jnp.int32),
        ],
        compiler_params=pltpu.CompilerParams(vmem_limit_bytes=60 * 1024 * 1024),
    )(station, block, templates)


def member_after(member, step):
    return (member // Y + step[0]) % X * Y + (member % Y + step[1]) % Y


def route_kernel(held_ref, ready_ref, *refs):
    sources = held_ref.shape[0]
    sent_refs, (tables, staged, chosen_ref, sem) = refs[:PLANE], refs[PLANE:]
    me = lax.axis_index("wide") % PLANE
    last = held_ref.shape[1] - 1
    tables[...] = to_f32(held_ref[:, last])
    entries = jnp.concatenate([held_ref[source, last] for source in range(sources)], axis=0)
    read_scalars(entries, ((0, 1),), staged, chosen_ref, sem).wait()
    lane, row = lanes_of((16, 128)), rows_of((16, 128))
    marked = (row == 14) & (lane >= 48) & (lane < 50)
    for step, sent_ref in zip(PLANE_STEPS, sent_refs):
        first = member_after(me, step) * CAP
        for source in range(sources):
            for j in range(CAP):
                chosen = chosen_ref[0, source * UNIT + first + j]
                slot = source * CAP + j
                sent_ref[slot, 0:16, :] = held_ref[source, chosen, 0:16, :]
                upper = to_f32(held_ref[source, chosen, 16:32, :])
                entry = jnp.broadcast_to(tables[source, pl.ds(first + j, 1), :], (16, 128))
                sent_ref[slot, 16:32, :] = to_bf16(jnp.where(marked, entry, upper))


def route(held, ready):
    sources = held.shape[0]
    vmem = pl.BlockSpec(memory_space=pltpu.VMEM)
    return pl.pallas_call(
        route_kernel,
        out_shape=[jax.ShapeDtypeStruct((sources * CAP, UNIT, 128), jnp.bfloat16)] * PLANE,
        in_specs=[vmem, pl.BlockSpec(memory_space=pl.ANY)],
        out_specs=[vmem] * PLANE,
        scratch_shapes=[
            pltpu.VMEM((sources, UNIT, 128), jnp.float32),
            pltpu.VMEM((8, sources * UNIT), jnp.int32),
            pltpu.SMEM((8, sources * UNIT), jnp.int32),
            pltpu.SemaphoreType.DMA,
        ],
        compiler_params=pltpu.CompilerParams(vmem_limit_bytes=VMEM_LIMIT),
        cost_estimate=pl.CostEstimate(flops=10_000_000_000, bytes_accessed=40_000_000, transcendentals=0),
    )(held, ready)


def station_kernel(wave_ref, tail_ref, shifted_ref, inverse_ref, signal, stacked):
    segment = wave_ref.shape[2]
    blocks = inverse_ref.shape[1]
    pieces = shifted_ref.shape[1]
    signal[CH:16, :] = jnp.zeros_like(signal[CH:16, :])
    signal[0:CH, 0:segment] = to_f32(wave_ref[0])
    signal[0:CH, segment:] = to_f32(tail_ref[0])
    lane, row = lanes_of((SHIFTS, 128)), rows_of((SHIFTS, 128))
    source = (lane + 8 * row) & 127
    inside = lane + 8 * row < 128

    for c in range(CH):
        before = None
        for piece in range(pieces + 1):
            here = jnp.broadcast_to(signal[c : c + 1, 128 * piece : 128 * piece + 128], (SHIFTS, 128))
            here = jnp.take_along_axis(here, source, axis=1)
            if piece > 0:
                shifted_ref[0, piece - 1, c] = to_bf16(jnp.where(inside, before, here))
            before = here
    for b in range(blocks):
        stacked[16 * b : 16 * b + 16, :] = signal[:, 128 * b : 128 * b + 512]
    sample, position = rows_of((512, 128)), lanes_of((512, 128))
    band = to_bf16(jnp.where((sample >= position) & (sample < position + L), 1.0, 0.0))
    values = stacked[...]
    squares = values * values
    high = to_bf16(squares)
    low = to_bf16(squares - to_f32(high))
    first = jnp.dot(to_bf16(values), band, preferred_element_type=jnp.float32) / L
    second = (
        jnp.dot(high, band, preferred_element_type=jnp.float32)
        + jnp.dot(low, band, preferred_element_type=jnp.float32)
    ) / L
    inverse = 1.0 / jnp.sqrt(second - first * first + EPS)
    inverse_ref[0] = inverse.reshape(blocks, 16, 128)


def station_tables(wave, tail):
    stations, channels, segment = wave.shape
    blocks = segment // BLK
    extra = tail.shape[2]
    return pl.pallas_call(
        station_kernel,
        grid=(stations,),
        out_shape=(
            jax.ShapeDtypeStruct((stations, blocks + 2, channels, SHIFTS, 128), jnp.bfloat16),
            jax.ShapeDtypeStruct((stations, blocks, 16, 128), jnp.float32),
        ),
        in_specs=[
            pl.BlockSpec((1, channels, segment), lambda s: (s, 0, 0)),
            pl.BlockSpec((1, channels, extra), lambda s: (s, 0, 0)),
        ],
        out_specs=(
            pl.BlockSpec((1, blocks + 2, channels, SHIFTS, 128), lambda s: (s, 0, 0, 0, 0)),
            pl.BlockSpec((1, blocks, 16, 128), lambda s: (s, 0, 0, 0)),
        ),
        scratch_shapes=[
            pltpu.VMEM((16, segment + extra), jnp.float32),
            pltpu.VMEM((16 * blocks, 512), jnp.float32),
        ],
        compiler_params=pltpu.CompilerParams(vmem_limit_bytes=VMEM_LIMIT),
        cost_estimate=pl.CostEstimate(flops=3_000_000_000, bytes_accessed=20_000_000, transcendentals=500_000),
    )(wave, tail)


def score_kernel(
    first_ref, second_ref, shifted_ref, inverse_ref, scores_ref, rows, marked, staged, codes, sem
):
    lane, row = lanes_of((8, 128)), rows_of((8, 128))
    before = lane < row
    member = lane // SHIFTS
    inverse_source = 8 * (lane % SHIFTS) + row
    natural_source = SHIFTS * row + lane // 8
    expand = to_bf16(jnp.where(lanes_of((GROUP, 256)) // SHIFTS == rows_of((GROUP, 256)), 1.0, 0.0))
    count = first_ref.shape[0]
    for start, units_ref in ((0, first_ref), (count, second_ref)):
        marked[start : start + count] = units_ref[:, 30, :]
    copy = read_scalars(marked[...], ((48, 32), (49, 1)), staged, codes, sem)
    for start, units_ref in ((0, first_ref), (count, second_ref)):
        units = units_ref[...]
        third = to_f32(units[:, 16:32, :])[:, 8:16, :]
        low_half = lanes_of(third.shape) < 64
        rows[start : start + count, 0:24, :] = to_f32(units)[:, 0:24, :]
        rows[start : start + count, 24:32, :] = jnp.where(low_half, third, 0.0)
        rows[start : start + count, 32:40, :] = jnp.where(low_half, pltpu.roll(third, 64, 2), 0.0)
    copy.wait()

    def template_rows(g, c):
        turned = []
        for r in (c, 12 + c, 24 + c if c < 6 else 26 + c):
            part = jnp.broadcast_to(rows[g, r : r + 1, :], (8, 128))
            turned.append(pltpu.roll(part, 0, 1, stride=1, stride_axis=0))
        return [
            jnp.where(before, 0.0, turned[0]),
            jnp.where(before, turned[0], turned[1]),
            jnp.where(before, turned[1], turned[2]),
        ]

    def score(group, carry):
        base = pl.multiple_of(group * GROUP, GROUP)
        marks = marked[pl.ds(base, GROUP), :]
        spread = lax.dot_general(marks, expand, TN, preferred_element_type=jnp.float32)
        factors = spread[0:12] + spread[16:28] + spread[32:44]
        totals = [jnp.zeros((8, 128), jnp.float32) for _ in range(2)]
        places = [(codes[0, base + g] // 32, codes[0, base + g] % 32) for g in range(GROUP)]
        for c in range(CH):
            pairs = []
            for pair in range(GROUP // 2):
                one, two = template_rows(base + 2 * pair, c), template_rows(base + 2 * pair + 1, c)
                both = [to_bf16(jnp.concatenate([one[a], two[a]], axis=0)) for a in range(3)]
                pairs.append(jnp.concatenate(both, axis=1))
            products = lax.dot_general(
                jnp.concatenate(pairs, axis=0),
                jnp.concatenate(
                    [
                        jnp.concatenate([shifted_ref[s, b + a, c] for s, b in places], axis=0)
                        for a in range(3)
                    ],
                    axis=1,
                ),
                NT,
                preferred_element_type=jnp.float32,
            )
            for half in range(2):
                chosen = jnp.zeros((8, 128), jnp.float32)
                scale = jnp.zeros((8, 128), jnp.float32)
                for m in range(8):
                    g = 8 * half + m
                    station, block = places[g]
                    inverse = jnp.broadcast_to(inverse_ref[station, block, c : c + 1, :], (8, 128))
                    inverse = jnp.take_along_axis(inverse, inverse_source, axis=1)
                    mine = products[8 * g : 8 * g + 8, 128 * half : 128 * half + 128]
                    chosen = jnp.where(member == m, mine, chosen)
                    scale = jnp.where(member == m, inverse, scale)
                factor = factors[c : c + 1, 128 * half : 128 * half + 128]
                totals[half] = totals[half] + chosen * scale * factor
        for half in range(2):
            natural = jnp.zeros((8, 128), jnp.float32)
            for i in range(8):
                spread_row = jnp.broadcast_to(totals[half][i : i + 1], (8, 128))
                spread_row = jnp.take_along_axis(spread_row, natural_source, axis=1)
                natural = jnp.where(lane % 8 == i, spread_row, natural)
            for o in range(2):
                scores_ref[group * 4 + half * 2 + o] = natural[4 * o : 4 * o + 4]
        return carry

    lax.fori_loop(0, 2 * count // GROUP, score, 0)


def slot_scores(first, second, shifted, inverse):
    slots = 2 * first.shape[0]
    vmem = pl.BlockSpec(memory_space=pltpu.VMEM)
    return pl.pallas_call(
        score_kernel,
        out_shape=jax.ShapeDtypeStruct((slots // CAP, CAP, BLK), jnp.float32),
        in_specs=[vmem] * 4,
        out_specs=vmem,
        scratch_shapes=[
            pltpu.VMEM((slots, 40, 128), jnp.float32),
            pltpu.VMEM((slots, 128), jnp.bfloat16),
            pltpu.VMEM((8, slots), jnp.int32),
            pltpu.SMEM((8, slots), jnp.int32),
            pltpu.SemaphoreType.DMA,
        ],
        compiler_params=pltpu.CompilerParams(vmem_limit_bytes=VMEM_LIMIT),
        cost_estimate=pl.CostEstimate(flops=4_000_000_000, bytes_accessed=4_000_000, transcendentals=0),
    )(first, second, shifted, inverse)


def arrange_kernel(*refs):
    scores_refs, out_ref = refs[:-1], refs[-1]
    me = lax.axis_index("wide") % PLANE
    planes = out_ref.shape[0] // PLANE
    for scores_ref, pair in zip(scores_refs, CALLS):
        for place, number in enumerate(pair):
            step = PLANE_STEPS[number]
            member = member_after(me, (X - step[0], Y - step[1]))
            for z in range(planes):
                out_ref[z * PLANE + member] = scores_ref[place * planes + z]


def arrange(scores):
    vmem = pl.BlockSpec(memory_space=pltpu.VMEM)
    return pl.pallas_call(
        arrange_kernel,
        out_shape=jax.ShapeDtypeStruct((len(scores) * scores[0].shape[0], CAP, BLK), jnp.float32),
        in_specs=[vmem] * len(scores),
        out_specs=vmem,
        compiler_params=pltpu.CompilerParams(vmem_limit_bytes=VMEM_LIMIT),
    )(*scores)


def unpack_kernel(place_ref, limit_ref, scores_ref, out_ref):
    templates, rows_part, _ = out_ref.shape
    for k in range(templates):
        for r in range(rows_part):
            slot = place_ref[k * rows_part + r]
            found = scores_ref[slot // CAP, pl.ds(slot % CAP, 1), :]
            out_ref[k, r : r + 1, :] = jnp.where(r < limit_ref[k], found, 0.0)


def unpack(place, limit, scores, shape):
    smem = pl.BlockSpec(memory_space=pltpu.SMEM)
    vmem = pl.BlockSpec(memory_space=pltpu.VMEM)
    return pl.pallas_call(
        unpack_kernel,
        out_shape=jax.ShapeDtypeStruct(shape, jnp.float32),
        in_specs=[smem, smem, vmem],
        out_specs=vmem,
        compiler_params=pltpu.CompilerParams(vmem_limit_bytes=VMEM_LIMIT),
    )(place, limit, scores)


def local(waveforms, templates, det_station, det_block, det_count):
    own_count, rows_part = det_station.shape
    wide_count = lax.axis_size("wide")
    narrow_count = lax.axis_size("narrow")
    planes = wide_count // PLANE
    members = [(z, p) for z in range(planes) for p in range(PLANE)]
    sent, place = pack(det_station, det_block, jnp.transpose(templates, (1, 0, 2)), wide_count)
    held = lax.all_to_all(
        sent.reshape(planes, (own_count + 1) * UNIT, 128),
        "wide",
        split_axis=0,
        concat_axis=0,
        tiled=True,
        axis_index_groups=[[PLANE * z + p for z in range(planes)] for p in range(PLANE)],
    )
    held = held.reshape(planes, own_count + 1, UNIT, 128)
    tail = lax.ppermute(
        waveforms[:, :, : 3 * BLK], "narrow", [(i, i - 1) for i in range(1, narrow_count)]
    )
    shifted, inverse = station_tables(waveforms, tail)
    routed = route(held, inverse)
    arrived = []
    for step, units in zip(PLANE_STEPS, routed):
        if step != (0, 0):
            pairs = [(PLANE * z + p, PLANE * z + member_after(p, step)) for z, p in members]
            units = lax.ppermute(units, "wide", pairs)
        arrived.append(units)
    scores = [slot_scores(arrived[a], arrived[b], shifted, inverse) for a, b in CALLS]
    returned = lax.all_to_all(arrange(scores), "wide", split_axis=0, concat_axis=0, tiled=True)
    limit = det_count - lax.axis_index("narrow") * rows_part
    return unpack(place, limit, returned, (own_count, rows_part, BLK))


def solution(mesh):
    placed = (
        P("wide", None, "narrow"),
        P("wide", None, None),
        P("wide", "narrow"),
        P("wide", "narrow"),
        P("wide"),
    )
    return jax.shard_map(
        local, mesh=mesh, in_specs=placed, out_specs=P("wide", "narrow", None), check_vma=False
    )
```

```python
import jax
import jax.numpy as jnp
from jax import lax
from jax.experimental import pallas as pl
from jax.experimental.pallas import tpu as pltpu
from jax.sharding import PartitionSpec as P

CH = 12
L = 300
BLK = 128
EPS = 1e-06
CAP = 4
UNIT = 32
PLANE = 8
X, Y = 4, 2
PLANE_STEPS = ((0, 0), (1, 0), (3, 0), (0, 1), (2, 0), (1, 1), (3, 1), (2, 1))
CALLS = ((6, 7), (4, 5), (2, 3), (0, 1))
SHIFTS = 16
GROUP = 16
VMEM_LIMIT = 24 * 1024 * 1024
NT = (((1,), (1,)), ((), ()))
TN = (((0,), (0,)), ((), ()))


def lanes_of(shape):
    return lax.broadcasted_iota(jnp.int32, shape, len(shape) - 1)


def rows_of(shape):
    return lax.broadcasted_iota(jnp.int32, shape, len(shape) - 2)


def to_bf16(values):
    return values.astype(jnp.bfloat16)


def to_f32(values):
    return values.astype(jnp.float32)


def read_scalars(rows, weights, staged, scalars, sem):
    lane = lanes_of((8, 128))
    picked = jnp.zeros((8, 128), jnp.float32)
    for place, weight in weights:
        picked = jnp.where(lane == place, float(weight), picked)
    values = lax.dot_general(to_bf16(picked), rows, NT, preferred_element_type=jnp.float32)
    staged[...] = values.astype(jnp.int32)
    copy = pltpu.make_async_copy(staged, scalars, sem)
    copy.start()
    return copy


def pack_kernel(station_ref, block_ref, templates_ref, sent_ref, place_ref, padded, units, table, used):
    channels, templates, _ = templates_ref.shape
    rows_part = station_ref.shape[1]
    values = to_f32(templates_ref[...])
    centred = values - jnp.sum(values, axis=2, keepdims=True) / L
    power = jnp.sum(centred * centred, axis=2, keepdims=True) / L
    factor = 1.0 / (60.0 * jnp.sqrt(power + EPS))
    padded[...] = jnp.zeros_like(padded)
    padded[:, :, 0:L] = to_f32(to_bf16(centred))
    high = to_f32(to_bf16(factor))
    middle = to_f32(to_bf16(factor - high))
    low = to_f32(to_bf16(factor - high - middle))
    lane = lanes_of((templates, 128))
    marks = jnp.zeros((templates, 128), jnp.float32)
    for c in range(channels):
        marks = jnp.where(lane == c, high[c], marks)
        marks = jnp.where(lane == c + 16, middle[c], marks)
        marks = jnp.where(lane == c + 32, low[c], marks)
        units[:, c, :] = padded[c, :, 0:128]
        units[:, 12 + c, :] = padded[c, :, 128:256]
    for c in range(6):
        units[:, 24 + c, :] = padded[c, :, 256:384] + pltpu.roll(padded[c + 6, :, 256:384], 64, 1)
    units[:, 30, :] = marks
    units[:, 31, :] = jnp.zeros_like(marks)
    for z in range(sent_ref.shape[0]):
        sent_ref[z, 0:templates] = to_bf16(units[...])
    table[...] = jnp.zeros_like(table)

    def clear(h, carry):
        used[h] = 0
        return carry

    lax.fori_loop(0, used.shape[0], clear, 0, unroll=8)
    lane = lanes_of((1, 128))

    def place(k, r):
        station = station_ref[k, r]
        block = block_ref[k, r] & 31
        holder = station >> 3
        rank = jnp.minimum(used[holder], CAP - 1)
        used[holder] = rank + 1
        slot = holder * CAP + rank
        place_ref[k * rows_part + r] = slot
        entry = jnp.where(lane == 0, k, jnp.where(lane == 48, station & 7, jnp.where(lane == 49, block, 0)))
        table[pl.ds(slot, 1), :] = to_f32(entry)

    for k in range(templates):
        for r in range(rows_part):
            place(k, r)
    for z in range(sent_ref.shape[0]):
        sent_ref[z, templates] = to_bf16(table[UNIT * z : UNIT * z + UNIT, :])


def pack(station, block, templates, holders):
    channels, count, _ = templates.shape
    smem = pl.BlockSpec(memory_space=pltpu.SMEM)
    vmem = pl.BlockSpec(memory_space=pltpu.VMEM)
    return pl.pallas_call(
        pack_kernel,
        out_shape=(
            jax.ShapeDtypeStruct((holders // PLANE, count + 1, UNIT, 128), jnp.bfloat16),
            jax.ShapeDtypeStruct((count * station.shape[1],), jnp.int32),
        ),
        in_specs=[smem, smem, vmem],
        out_specs=(vmem, smem),
        scratch_shapes=[
            pltpu.VMEM((channels, count, 384), jnp.float32),
            pltpu.VMEM((count, UNIT, 128), jnp.float32),
            pltpu.VMEM((holders * CAP, 128), jnp.float32),
            pltpu.SMEM((holders,), jnp.int32),
        ],
        compiler_params=pltpu.CompilerParams(vmem_limit_bytes=60 * 1024 * 1024),
    )(station, block, templates)


def member_after(member, step):
    return (member // Y + step[0]) % X * Y + (member % Y + step[1]) % Y


def route_kernel(held_ref, ready_ref, *refs):
    sources = held_ref.shape[0]
    sent_refs, (tables, staged, chosen_ref, sem) = refs[:PLANE], refs[PLANE:]
    me = lax.axis_index("wide") % PLANE
    last = held_ref.shape[1] - 1
    tables[...] = to_f32(held_ref[:, last])
    entries = jnp.concatenate([held_ref[source, last] for source in range(sources)], axis=0)
    read_scalars(entries, ((0, 1),), staged, chosen_ref, sem).wait()
    lane, row = lanes_of((16, 128)), rows_of((16, 128))
    marked = (row == 14) & (lane >= 48) & (lane < 50)
    for step, sent_ref in zip(PLANE_STEPS, sent_refs):
        first = member_after(me, step) * CAP
        for source in range(sources):
            for j in range(CAP):
                chosen = chosen_ref[0, source * UNIT + first + j]
                slot = source * CAP + j
                sent_ref[slot, 0:16, :] = held_ref[source, chosen, 0:16, :]
                upper = to_f32(held_ref[source, chosen, 16:32, :])
                entry = jnp.broadcast_to(tables[source, pl.ds(first + j, 1), :], (16, 128))
                sent_ref[slot, 16:32, :] = to_bf16(jnp.where(marked, entry, upper))


def route(held, ready):
    sources = held.shape[0]
    vmem = pl.BlockSpec(memory_space=pltpu.VMEM)
    return pl.pallas_call(
        route_kernel,
        out_shape=[jax.ShapeDtypeStruct((sources * CAP, UNIT, 128), jnp.bfloat16)] * PLANE,
        in_specs=[vmem, pl.BlockSpec(memory_space=pl.ANY)],
        out_specs=[vmem] * PLANE,
        scratch_shapes=[
            pltpu.VMEM((sources, UNIT, 128), jnp.float32),
            pltpu.VMEM((8, sources * UNIT), jnp.int32),
            pltpu.SMEM((8, sources * UNIT), jnp.int32),
            pltpu.SemaphoreType.DMA,
        ],
        compiler_params=pltpu.CompilerParams(vmem_limit_bytes=VMEM_LIMIT),
        cost_estimate=pl.CostEstimate(flops=10_000_000_000, bytes_accessed=40_000_000, transcendentals=0),
    )(held, ready)


def station_kernel(wave_ref, tail_ref, shifted_ref, inverse_ref, signal, stacked):
    segment = wave_ref.shape[2]
    blocks = inverse_ref.shape[1]
    pieces = shifted_ref.shape[1]
    signal[CH:16, :] = jnp.zeros_like(signal[CH:16, :])
    signal[0:CH, 0:segment] = to_f32(wave_ref[0])
    signal[0:CH, segment:] = to_f32(tail_ref[0])
    lane, row = lanes_of((SHIFTS, 128)), rows_of((SHIFTS, 128))
    source = (lane + 8 * row) & 127
    inside = lane + 8 * row < 128

    for c in range(CH):
        before = None
        for piece in range(pieces + 1):
            here = jnp.broadcast_to(signal[c : c + 1, 128 * piece : 128 * piece + 128], (SHIFTS, 128))
            here = jnp.take_along_axis(here, source, axis=1)
            if piece > 0:
                shifted_ref[0, piece - 1, c] = to_bf16(jnp.where(inside, before, here))
            before = here
    for b in range(blocks):
        stacked[16 * b : 16 * b + 16, :] = signal[:, 128 * b : 128 * b + 512]
    sample, position = rows_of((512, 128)), lanes_of((512, 128))
    band = to_bf16(jnp.where((sample >= position) & (sample < position + L), 1.0, 0.0))
    values = stacked[...]
    squares = values * values
    high = to_bf16(squares)
    low = to_bf16(squares - to_f32(high))
    first = jnp.dot(to_bf16(values), band, preferred_element_type=jnp.float32) / L
    second = (
        jnp.dot(high, band, preferred_element_type=jnp.float32)
        + jnp.dot(low, band, preferred_element_type=jnp.float32)
    ) / L
    inverse = 1.0 / jnp.sqrt(second - first * first + EPS)
    inverse_ref[0] = inverse.reshape(blocks, 16, 128)


def station_tables(wave, tail):
    stations, channels, segment = wave.shape
    blocks = segment // BLK
    extra = tail.shape[2]
    return pl.pallas_call(
        station_kernel,
        grid=(stations,),
        out_shape=(
            jax.ShapeDtypeStruct((stations, blocks + 2, channels, SHIFTS, 128), jnp.bfloat16),
            jax.ShapeDtypeStruct((stations, blocks, 16, 128), jnp.float32),
        ),
        in_specs=[
            pl.BlockSpec((1, channels, segment), lambda s: (s, 0, 0)),
            pl.BlockSpec((1, channels, extra), lambda s: (s, 0, 0)),
        ],
        out_specs=(
            pl.BlockSpec((1, blocks + 2, channels, SHIFTS, 128), lambda s: (s, 0, 0, 0, 0)),
            pl.BlockSpec((1, blocks, 16, 128), lambda s: (s, 0, 0, 0)),
        ),
        scratch_shapes=[
            pltpu.VMEM((16, segment + extra), jnp.float32),
            pltpu.VMEM((16 * blocks, 512), jnp.float32),
        ],
        compiler_params=pltpu.CompilerParams(vmem_limit_bytes=VMEM_LIMIT),
        cost_estimate=pl.CostEstimate(flops=3_000_000_000, bytes_accessed=20_000_000, transcendentals=500_000),
    )(wave, tail)


def score_kernel(
    first_ref, second_ref, shifted_ref, inverse_ref, scores_ref, rows, marked, staged, codes, sem
):
    lane, row = lanes_of((8, 128)), rows_of((8, 128))
    before = lane < row
    member = lane // SHIFTS
    inverse_source = 8 * (lane % SHIFTS) + row
    natural_source = SHIFTS * row + lane // 8
    expand = to_bf16(jnp.where(lanes_of((GROUP, 256)) // SHIFTS == rows_of((GROUP, 256)), 1.0, 0.0))
    count = first_ref.shape[0]
    for start, units_ref in ((0, first_ref), (count, second_ref)):
        marked[start : start + count] = units_ref[:, 30, :]
    copy = read_scalars(marked[...], ((48, 32), (49, 1)), staged, codes, sem)
    for start, units_ref in ((0, first_ref), (count, second_ref)):
        units = units_ref[...]
        third = to_f32(units[:, 16:32, :])[:, 8:16, :]
        low_half = lanes_of(third.shape) < 64
        rows[start : start + count, 0:24, :] = to_f32(units)[:, 0:24, :]
        rows[start : start + count, 24:32, :] = jnp.where(low_half, third, 0.0)
        rows[start : start + count, 32:40, :] = jnp.where(low_half, pltpu.roll(third, 64, 2), 0.0)
    copy.wait()

    def template_rows(g, c):
        turned = []
        for r in (c, 12 + c, 24 + c if c < 6 else 26 + c):
            part = jnp.broadcast_to(rows[g, r : r + 1, :], (8, 128))
            turned.append(pltpu.roll(part, 0, 1, stride=1, stride_axis=0))
        return [
            jnp.where(before, 0.0, turned[0]),
            jnp.where(before, turned[0], turned[1]),
            jnp.where(before, turned[1], turned[2]),
        ]

    def score(group, carry):
        base = pl.multiple_of(group * GROUP, GROUP)
        marks = marked[pl.ds(base, GROUP), :]
        spread = lax.dot_general(marks, expand, TN, preferred_element_type=jnp.float32)
        factors = spread[0:12] + spread[16:28] + spread[32:44]
        totals = [jnp.zeros((8, 128), jnp.float32) for _ in range(2)]
        places = [(codes[0, base + g] >> 5, codes[0, base + g] & 31) for g in range(GROUP)]
        for c in range(CH):
            pairs = []
            for pair in range(GROUP // 2):
                one, two = template_rows(base + 2 * pair, c), template_rows(base + 2 * pair + 1, c)
                both = [to_bf16(jnp.concatenate([one[a], two[a]], axis=0)) for a in range(3)]
                pairs.append(jnp.concatenate(both, axis=1))
            products = lax.dot_general(
                jnp.concatenate(pairs, axis=0),
                jnp.concatenate(
                    [
                        jnp.concatenate([shifted_ref[s, b + a, c] for s, b in places], axis=0)
                        for a in range(3)
                    ],
                    axis=1,
                ),
                NT,
                preferred_element_type=jnp.float32,
            )
            for half in range(2):
                chosen = jnp.zeros((8, 128), jnp.float32)
                scale = jnp.zeros((8, 128), jnp.float32)
                for m in range(8):
                    g = 8 * half + m
                    station, block = places[g]
                    inverse = jnp.broadcast_to(inverse_ref[station, block, c : c + 1, :], (8, 128))
                    inverse = jnp.take_along_axis(inverse, inverse_source, axis=1)
                    mine = products[8 * g : 8 * g + 8, 128 * half : 128 * half + 128]
                    chosen = jnp.where(member == m, mine, chosen)
                    scale = jnp.where(member == m, inverse, scale)
                factor = factors[c : c + 1, 128 * half : 128 * half + 128]
                totals[half] = totals[half] + chosen * scale * factor
        for half in range(2):
            natural = jnp.zeros((8, 128), jnp.float32)
            for i in range(8):
                spread_row = jnp.broadcast_to(totals[half][i : i + 1], (8, 128))
                spread_row = jnp.take_along_axis(spread_row, natural_source, axis=1)
                natural = jnp.where(lane % 8 == i, spread_row, natural)
            for o in range(2):
                scores_ref[group * 4 + half * 2 + o] = natural[4 * o : 4 * o + 4]
        return carry

    lax.fori_loop(0, 2 * count // GROUP, score, 0)


def slot_scores(first, second, shifted, inverse):
    slots = 2 * first.shape[0]
    vmem = pl.BlockSpec(memory_space=pltpu.VMEM)
    return pl.pallas_call(
        score_kernel,
        out_shape=jax.ShapeDtypeStruct((slots // CAP, CAP, BLK), jnp.float32),
        in_specs=[vmem] * 4,
        out_specs=vmem,
        scratch_shapes=[
            pltpu.VMEM((slots, 40, 128), jnp.float32),
            pltpu.VMEM((slots, 128), jnp.bfloat16),
            pltpu.VMEM((8, slots), jnp.int32),
            pltpu.SMEM((8, slots), jnp.int32),
            pltpu.SemaphoreType.DMA,
        ],
        compiler_params=pltpu.CompilerParams(vmem_limit_bytes=VMEM_LIMIT),
        cost_estimate=pl.CostEstimate(flops=4_000_000_000, bytes_accessed=4_000_000, transcendentals=0),
    )(first, second, shifted, inverse)


def arrange_kernel(*refs):
    scores_refs, out_ref = refs[:-1], refs[-1]
    me = lax.axis_index("wide") % PLANE
    planes = out_ref.shape[0] // PLANE
    for scores_ref, pair in zip(scores_refs, CALLS):
        for place, number in enumerate(pair):
            step = PLANE_STEPS[number]
            member = member_after(me, (X - step[0], Y - step[1]))
            for z in range(planes):
                out_ref[z * PLANE + member] = scores_ref[place * planes + z]


def arrange(scores):
    vmem = pl.BlockSpec(memory_space=pltpu.VMEM)
    return pl.pallas_call(
        arrange_kernel,
        out_shape=jax.ShapeDtypeStruct((len(scores) * scores[0].shape[0], CAP, BLK), jnp.float32),
        in_specs=[vmem] * len(scores),
        out_specs=vmem,
        compiler_params=pltpu.CompilerParams(vmem_limit_bytes=VMEM_LIMIT),
    )(*scores)


def unpack_kernel(place_ref, limit_ref, scores_ref, out_ref):
    templates, rows_part, _ = out_ref.shape
    for k in range(templates):
        for r in range(rows_part):
            slot = place_ref[k * rows_part + r]
            found = scores_ref[slot >> 2, pl.ds(slot & 3, 1), :]
            out_ref[k, r : r + 1, :] = jnp.where(r < limit_ref[k], found, 0.0)


def unpack(place, limit, scores, shape):
    smem = pl.BlockSpec(memory_space=pltpu.SMEM)
    vmem = pl.BlockSpec(memory_space=pltpu.VMEM)
    return pl.pallas_call(
        unpack_kernel,
        out_shape=jax.ShapeDtypeStruct(shape, jnp.float32),
        in_specs=[smem, smem, vmem],
        out_specs=vmem,
        compiler_params=pltpu.CompilerParams(vmem_limit_bytes=VMEM_LIMIT),
    )(place, limit, scores)


def local(waveforms, templates, det_station, det_block, det_count):
    own_count, rows_part = det_station.shape
    wide_count = lax.axis_size("wide")
    narrow_count = lax.axis_size("narrow")
    planes = wide_count // PLANE
    members = [(z, p) for z in range(planes) for p in range(PLANE)]
    sent, place = pack(det_station, det_block, jnp.transpose(templates, (1, 0, 2)), wide_count)
    held = lax.all_to_all(
        sent.reshape(planes, (own_count + 1) * UNIT, 128),
        "wide",
        split_axis=0,
        concat_axis=0,
        tiled=True,
        axis_index_groups=[[PLANE * z + p for z in range(planes)] for p in range(PLANE)],
    )
    held = held.reshape(planes, own_count + 1, UNIT, 128)
    tail = lax.ppermute(
        waveforms[:, :, : 3 * BLK], "narrow", [(i, i - 1) for i in range(1, narrow_count)]
    )
    shifted, inverse = station_tables(waveforms, tail)
    routed = route(held, inverse)
    arrived = []
    for step, units in zip(PLANE_STEPS, routed):
        if step != (0, 0):
            pairs = [(PLANE * z + p, PLANE * z + member_after(p, step)) for z, p in members]
            units = lax.ppermute(units, "wide", pairs)
        arrived.append(units)
    scores = [slot_scores(arrived[a], arrived[b], shifted, inverse) for a, b in CALLS]
    returned = lax.all_to_all(arrange(scores), "wide", split_axis=0, concat_axis=0, tiled=True)
    limit = det_count - lax.axis_index("narrow") * rows_part
    return unpack(place, limit, returned, (own_count, rows_part, BLK))


def solution(mesh):
    placed = (
        P("wide", None, "narrow"),
        P("wide", None, None),
        P("wide", "narrow"),
        P("wide", "narrow"),
        P("wide"),
    )
    return jax.shard_map(
        local, mesh=mesh, in_specs=placed, out_specs=P("wide", "narrow", None), check_vma=False
    )
```

```python
import jax
import jax.numpy as jnp
from jax import lax
from jax.experimental import pallas as pl
from jax.experimental.pallas import tpu as pltpu
from jax.sharding import PartitionSpec as P

CH = 12
L = 300
BLK = 128
EPS = 1e-06
CAP = 4
UNIT = 32
PLANE = 8
X, Y = 4, 2
PLANE_STEPS = ((0, 0), (1, 0), (3, 0), (0, 1), (2, 0), (1, 1), (3, 1), (2, 1))
CALLS = ((0, 1), (2, 3), (4, 5), (6, 7))
HELD_BACK = ((6, 7), (), (), ())
SHIFTS = 16
GROUP = 16
VMEM_LIMIT = 24 * 1024 * 1024
NT = (((1,), (1,)), ((), ()))
TN = (((0,), (0,)), ((), ()))


def lanes_of(shape):
    return lax.broadcasted_iota(jnp.int32, shape, len(shape) - 1)


def rows_of(shape):
    return lax.broadcasted_iota(jnp.int32, shape, len(shape) - 2)


def to_bf16(values):
    return values.astype(jnp.bfloat16)


def to_f32(values):
    return values.astype(jnp.float32)


def read_scalars(rows, weights, staged, scalars, sem):
    lane = lanes_of((8, 128))
    picked = jnp.zeros((8, 128), jnp.float32)
    for place, weight in weights:
        picked = jnp.where(lane == place, float(weight), picked)
    values = lax.dot_general(to_bf16(picked), rows, NT, preferred_element_type=jnp.float32)
    staged[...] = values.astype(jnp.int32)
    copy = pltpu.make_async_copy(staged, scalars, sem)
    copy.start()
    return copy


def pack_kernel(station_ref, block_ref, templates_ref, sent_ref, place_ref, padded, units, table, used):
    channels, templates, _ = templates_ref.shape
    rows_part = station_ref.shape[1]
    values = to_f32(templates_ref[...])
    centred = values - jnp.sum(values, axis=2, keepdims=True) / L
    power = jnp.sum(centred * centred, axis=2, keepdims=True) / L
    factor = 1.0 / (60.0 * jnp.sqrt(power + EPS))
    padded[...] = jnp.zeros_like(padded)
    padded[:, :, 0:L] = to_f32(to_bf16(centred))
    high = to_f32(to_bf16(factor))
    middle = to_f32(to_bf16(factor - high))
    low = to_f32(to_bf16(factor - high - middle))
    lane = lanes_of((templates, 128))
    marks = jnp.zeros((templates, 128), jnp.float32)
    for c in range(channels):
        marks = jnp.where(lane == c, high[c], marks)
        marks = jnp.where(lane == c + 16, middle[c], marks)
        marks = jnp.where(lane == c + 32, low[c], marks)
        units[:, c, :] = padded[c, :, 0:128]
        units[:, 12 + c, :] = padded[c, :, 128:256]
    for c in range(6):
        units[:, 24 + c, :] = padded[c, :, 256:384] + pltpu.roll(padded[c + 6, :, 256:384], 64, 1)
    units[:, 30, :] = marks
    units[:, 31, :] = jnp.zeros_like(marks)
    for z in range(sent_ref.shape[0]):
        sent_ref[z, 0:templates] = to_bf16(units[...])
    table[...] = jnp.zeros_like(table)

    def clear(h, carry):
        used[h] = 0
        return carry

    lax.fori_loop(0, used.shape[0], clear, 0, unroll=8)
    lane = lanes_of((1, 128))

    def place(k, r):
        station = station_ref[k, r]
        block = block_ref[k, r] & 31
        holder = station >> 3
        rank = jnp.minimum(used[holder], CAP - 1)
        used[holder] = rank + 1
        slot = holder * CAP + rank
        place_ref[k * rows_part + r] = slot
        entry = jnp.where(lane == 0, k, jnp.where(lane == 48, station & 7, jnp.where(lane == 49, block, 0)))
        table[pl.ds(slot, 1), :] = to_f32(entry)

    for k in range(templates):
        for r in range(rows_part):
            place(k, r)
    for z in range(sent_ref.shape[0]):
        sent_ref[z, templates] = to_bf16(table[UNIT * z : UNIT * z + UNIT, :])


def pack(station, block, templates, holders):
    channels, count, _ = templates.shape
    smem = pl.BlockSpec(memory_space=pltpu.SMEM)
    vmem = pl.BlockSpec(memory_space=pltpu.VMEM)
    return pl.pallas_call(
        pack_kernel,
        out_shape=(
            jax.ShapeDtypeStruct((holders // PLANE, count + 1, UNIT, 128), jnp.bfloat16),
            jax.ShapeDtypeStruct((count * station.shape[1],), jnp.int32),
        ),
        in_specs=[smem, smem, vmem],
        out_specs=(vmem, smem),
        scratch_shapes=[
            pltpu.VMEM((channels, count, 384), jnp.float32),
            pltpu.VMEM((count, UNIT, 128), jnp.float32),
            pltpu.VMEM((holders * CAP, 128), jnp.float32),
            pltpu.SMEM((holders,), jnp.int32),
        ],
        compiler_params=pltpu.CompilerParams(vmem_limit_bytes=60 * 1024 * 1024),
    )(station, block, templates)


def member_after(member, step):
    return (member // Y + step[0]) % X * Y + (member % Y + step[1]) % Y


def route_kernel(held_ref, ready_ref, *refs):
    sources = held_ref.shape[0]
    sent_refs, (tables, staged, chosen_ref, sem) = refs[:PLANE], refs[PLANE:]
    me = lax.axis_index("wide") % PLANE
    last = held_ref.shape[1] - 1
    tables[...] = to_f32(held_ref[:, last])
    entries = jnp.concatenate([held_ref[source, last] for source in range(sources)], axis=0)
    read_scalars(entries, ((0, 1),), staged, chosen_ref, sem).wait()
    lane, row = lanes_of((16, 128)), rows_of((16, 128))
    marked = (row == 14) & (lane >= 48) & (lane < 50)
    for step, sent_ref in zip(PLANE_STEPS, sent_refs):
        first = member_after(me, step) * CAP
        for source in range(sources):
            for j in range(CAP):
                chosen = chosen_ref[0, source * UNIT + first + j]
                slot = source * CAP + j
                sent_ref[slot, 0:16, :] = held_ref[source, chosen, 0:16, :]
                upper = to_f32(held_ref[source, chosen, 16:32, :])
                entry = jnp.broadcast_to(tables[source, pl.ds(first + j, 1), :], (16, 128))
                sent_ref[slot, 16:32, :] = to_bf16(jnp.where(marked, entry, upper))


def route(held, ready):
    sources = held.shape[0]
    vmem = pl.BlockSpec(memory_space=pltpu.VMEM)
    return pl.pallas_call(
        route_kernel,
        out_shape=[jax.ShapeDtypeStruct((sources * CAP, UNIT, 128), jnp.bfloat16)] * PLANE,
        in_specs=[vmem, pl.BlockSpec(memory_space=pl.ANY)],
        out_specs=[vmem] * PLANE,
        scratch_shapes=[
            pltpu.VMEM((sources, UNIT, 128), jnp.float32),
            pltpu.VMEM((8, sources * UNIT), jnp.int32),
            pltpu.SMEM((8, sources * UNIT), jnp.int32),
            pltpu.SemaphoreType.DMA,
        ],
        compiler_params=pltpu.CompilerParams(vmem_limit_bytes=VMEM_LIMIT),
        cost_estimate=pl.CostEstimate(flops=10_000_000_000, bytes_accessed=40_000_000, transcendentals=0),
    )(held, ready)


def station_kernel(wave_ref, tail_ref, shifted_ref, inverse_ref, signal, stacked):
    segment = wave_ref.shape[2]
    blocks = inverse_ref.shape[1]
    pieces = shifted_ref.shape[1]
    signal[CH:16, :] = jnp.zeros_like(signal[CH:16, :])
    signal[0:CH, 0:segment] = to_f32(wave_ref[0])
    signal[0:CH, segment:] = to_f32(tail_ref[0])
    lane, row = lanes_of((SHIFTS, 128)), rows_of((SHIFTS, 128))
    source = (lane + 8 * row) & 127
    inside = lane + 8 * row < 128

    for c in range(CH):
        before = None
        for piece in range(pieces + 1):
            here = jnp.broadcast_to(signal[c : c + 1, 128 * piece : 128 * piece + 128], (SHIFTS, 128))
            here = jnp.take_along_axis(here, source, axis=1)
            if piece > 0:
                shifted_ref[0, piece - 1, c] = to_bf16(jnp.where(inside, before, here))
            before = here
    for b in range(blocks):
        stacked[16 * b : 16 * b + 16, :] = signal[:, 128 * b : 128 * b + 512]
    sample, position = rows_of((512, 128)), lanes_of((512, 128))
    band = to_bf16(jnp.where((sample >= position) & (sample < position + L), 1.0, 0.0))
    values = stacked[...]
    squares = values * values
    high = to_bf16(squares)
    low = to_bf16(squares - to_f32(high))
    first = jnp.dot(to_bf16(values), band, preferred_element_type=jnp.float32) / L
    second = (
        jnp.dot(high, band, preferred_element_type=jnp.float32)
        + jnp.dot(low, band, preferred_element_type=jnp.float32)
    ) / L
    inverse = 1.0 / jnp.sqrt(second - first * first + EPS)
    inverse_ref[0] = inverse.reshape(blocks, 16, 128)


def station_tables(wave, tail):
    stations, channels, segment = wave.shape
    blocks = segment // BLK
    extra = tail.shape[2]
    return pl.pallas_call(
        station_kernel,
        grid=(stations,),
        out_shape=(
            jax.ShapeDtypeStruct((stations, blocks + 2, channels, SHIFTS, 128), jnp.bfloat16),
            jax.ShapeDtypeStruct((stations, blocks, 16, 128), jnp.float32),
        ),
        in_specs=[
            pl.BlockSpec((1, channels, segment), lambda s: (s, 0, 0)),
            pl.BlockSpec((1, channels, extra), lambda s: (s, 0, 0)),
        ],
        out_specs=(
            pl.BlockSpec((1, blocks + 2, channels, SHIFTS, 128), lambda s: (s, 0, 0, 0, 0)),
            pl.BlockSpec((1, blocks, 16, 128), lambda s: (s, 0, 0, 0)),
        ),
        scratch_shapes=[
            pltpu.VMEM((16, segment + extra), jnp.float32),
            pltpu.VMEM((16 * blocks, 512), jnp.float32),
        ],
        compiler_params=pltpu.CompilerParams(vmem_limit_bytes=VMEM_LIMIT),
        cost_estimate=pl.CostEstimate(flops=3_000_000_000, bytes_accessed=20_000_000, transcendentals=500_000),
    )(wave, tail)


def score_kernel(first_ref, second_ref, shifted_ref, inverse_ref, *refs):
    held_back = len(refs) // 2 - 3
    scores_ref, (rows, marked, staged, codes, sem) = refs[held_back], refs[-5:]
    lane, row = lanes_of((8, 128)), rows_of((8, 128))
    before = lane < row
    member = lane // SHIFTS
    inverse_source = 8 * (lane % SHIFTS) + row
    natural_source = SHIFTS * row + lane // 8
    expand = to_bf16(jnp.where(lanes_of((GROUP, 256)) // SHIFTS == rows_of((GROUP, 256)), 1.0, 0.0))
    count = first_ref.shape[0]
    for start, units_ref in ((0, first_ref), (count, second_ref)):
        marked[start : start + count] = units_ref[:, 30, :]
    copy = read_scalars(marked[...], ((48, 32), (49, 1)), staged, codes, sem)
    for start, units_ref in ((0, first_ref), (count, second_ref)):
        units = units_ref[...]
        third = to_f32(units[:, 16:32, :])[:, 8:16, :]
        low_half = lanes_of(third.shape) < 64
        rows[start : start + count, 0:24, :] = to_f32(units)[:, 0:24, :]
        rows[start : start + count, 24:32, :] = jnp.where(low_half, third, 0.0)
        rows[start : start + count, 32:40, :] = jnp.where(low_half, pltpu.roll(third, 64, 2), 0.0)
    copy.wait()

    def template_rows(g, c):
        turned = []
        for r in (c, 12 + c, 24 + c if c < 6 else 26 + c):
            part = jnp.broadcast_to(rows[g, r : r + 1, :], (8, 128))
            turned.append(pltpu.roll(part, 0, 1, stride=1, stride_axis=0))
        return [
            jnp.where(before, 0.0, turned[0]),
            jnp.where(before, turned[0], turned[1]),
            jnp.where(before, turned[1], turned[2]),
        ]

    def score(group, carry):
        base = pl.multiple_of(group * GROUP, GROUP)
        marks = marked[pl.ds(base, GROUP), :]
        spread = lax.dot_general(marks, expand, TN, preferred_element_type=jnp.float32)
        factors = spread[0:12] + spread[16:28] + spread[32:44]
        totals = [jnp.zeros((8, 128), jnp.float32) for _ in range(2)]
        places = [(codes[0, base + g] >> 5, codes[0, base + g] & 31) for g in range(GROUP)]
        for c in range(CH):
            pairs = []
            for pair in range(GROUP // 2):
                one, two = template_rows(base + 2 * pair, c), template_rows(base + 2 * pair + 1, c)
                both = [to_bf16(jnp.concatenate([one[a], two[a]], axis=0)) for a in range(3)]
                pairs.append(jnp.concatenate(both, axis=1))
            products = lax.dot_general(
                jnp.concatenate(pairs, axis=0),
                jnp.concatenate(
                    [
                        jnp.concatenate([shifted_ref[s, b + a, c] for s, b in places], axis=0)
                        for a in range(3)
                    ],
                    axis=1,
                ),
                NT,
                preferred_element_type=jnp.float32,
            )
            for half in range(2):
                chosen = jnp.zeros((8, 128), jnp.float32)
                scale = jnp.zeros((8, 128), jnp.float32)
                for m in range(8):
                    g = 8 * half + m
                    station, block = places[g]
                    inverse = jnp.broadcast_to(inverse_ref[station, block, c : c + 1, :], (8, 128))
                    inverse = jnp.take_along_axis(inverse, inverse_source, axis=1)
                    mine = products[8 * g : 8 * g + 8, 128 * half : 128 * half + 128]
                    chosen = jnp.where(member == m, mine, chosen)
                    scale = jnp.where(member == m, inverse, scale)
                factor = factors[c : c + 1, 128 * half : 128 * half + 128]
                totals[half] = totals[half] + chosen * scale * factor
        for half in range(2):
            natural = jnp.zeros((8, 128), jnp.float32)
            for i in range(8):
                spread_row = jnp.broadcast_to(totals[half][i : i + 1], (8, 128))
                spread_row = jnp.take_along_axis(spread_row, natural_source, axis=1)
                natural = jnp.where(lane % 8 == i, spread_row, natural)
            for o in range(2):
                scores_ref[group * 4 + half * 2 + o] = natural[4 * o : 4 * o + 4]
        return carry

    lax.fori_loop(0, 2 * count // GROUP, score, 0)


def slot_scores(first, second, shifted, inverse, held_back):
    anywhere = [pl.BlockSpec(memory_space=pl.ANY)] * len(held_back)
    slots = 2 * first.shape[0]
    vmem = pl.BlockSpec(memory_space=pltpu.VMEM)
    return pl.pallas_call(
        score_kernel,
        out_shape=[
            jax.ShapeDtypeStruct((slots // CAP, CAP, BLK), jnp.float32),
            *[jax.ShapeDtypeStruct(array.shape, array.dtype) for array in held_back],
        ],
        in_specs=[*[vmem] * 4, *anywhere],
        out_specs=[vmem, *anywhere],
        input_output_aliases={4 + i: 1 + i for i in range(len(held_back))},
        scratch_shapes=[
            pltpu.VMEM((slots, 40, 128), jnp.float32),
            pltpu.VMEM((slots, 128), jnp.bfloat16),
            pltpu.VMEM((8, slots), jnp.int32),
            pltpu.SMEM((8, slots), jnp.int32),
            pltpu.SemaphoreType.DMA,
        ],
        compiler_params=pltpu.CompilerParams(vmem_limit_bytes=VMEM_LIMIT),
        cost_estimate=pl.CostEstimate(flops=4_000_000_000, bytes_accessed=4_000_000, transcendentals=0),
    )(first, second, shifted, inverse, *held_back)


def arrange_kernel(*refs):
    scores_refs, out_ref = refs[:-1], refs[-1]
    me = lax.axis_index("wide") % PLANE
    planes = out_ref.shape[0] // PLANE
    for scores_ref, pair in zip(scores_refs, CALLS):
        for place, number in enumerate(pair):
            step = PLANE_STEPS[number]
            member = member_after(me, (X - step[0], Y - step[1]))
            for z in range(planes):
                out_ref[z * PLANE + member] = scores_ref[place * planes + z]


def arrange(scores):
    vmem = pl.BlockSpec(memory_space=pltpu.VMEM)
    return pl.pallas_call(
        arrange_kernel,
        out_shape=jax.ShapeDtypeStruct((len(scores) * scores[0].shape[0], CAP, BLK), jnp.float32),
        in_specs=[vmem] * len(scores),
        out_specs=vmem,
        compiler_params=pltpu.CompilerParams(vmem_limit_bytes=VMEM_LIMIT),
    )(*scores)


def unpack_kernel(place_ref, limit_ref, scores_ref, out_ref):
    templates, rows_part, _ = out_ref.shape
    for k in range(templates):
        for r in range(rows_part):
            slot = place_ref[k * rows_part + r]
            found = scores_ref[slot >> 2, pl.ds(slot & 3, 1), :]
            out_ref[k, r : r + 1, :] = jnp.where(r < limit_ref[k], found, 0.0)


def unpack(place, limit, scores, shape):
    smem = pl.BlockSpec(memory_space=pltpu.SMEM)
    vmem = pl.BlockSpec(memory_space=pltpu.VMEM)
    return pl.pallas_call(
        unpack_kernel,
        out_shape=jax.ShapeDtypeStruct(shape, jnp.float32),
        in_specs=[smem, smem, vmem],
        out_specs=vmem,
        compiler_params=pltpu.CompilerParams(vmem_limit_bytes=VMEM_LIMIT),
    )(place, limit, scores)


def local(waveforms, templates, det_station, det_block, det_count):
    own_count, rows_part = det_station.shape
    wide_count = lax.axis_size("wide")
    narrow_count = lax.axis_size("narrow")
    planes = wide_count // PLANE
    members = [(z, p) for z in range(planes) for p in range(PLANE)]
    sent, place = pack(det_station, det_block, jnp.transpose(templates, (1, 0, 2)), wide_count)
    held = lax.all_to_all(
        sent.reshape(planes, (own_count + 1) * UNIT, 128),
        "wide",
        split_axis=0,
        concat_axis=0,
        tiled=True,
        axis_index_groups=[[PLANE * z + p for z in range(planes)] for p in range(PLANE)],
    )
    held = held.reshape(planes, own_count + 1, UNIT, 128)
    tail = lax.ppermute(
        waveforms[:, :, : 3 * BLK], "narrow", [(i, i - 1) for i in range(1, narrow_count)]
    )
    shifted, inverse = station_tables(waveforms, tail)
    routed = route(held, inverse)
    routed = list(routed)
    scores = []
    for call, kept in zip(CALLS, HELD_BACK):
        units = []
        for number in call:
            value = routed[number]
            if number > 0:
                step = PLANE_STEPS[number]
                pairs = [(PLANE * z + p, PLANE * z + member_after(p, step)) for z, p in members]
                value = lax.ppermute(value, "wide", pairs)
            units.append(value)
        found, *passed = slot_scores(*units, shifted, inverse, [routed[number] for number in kept])
        for number, value in zip(kept, passed):
            routed[number] = value
        scores.append(found)
    returned = lax.all_to_all(arrange(scores), "wide", split_axis=0, concat_axis=0, tiled=True)
    limit = det_count - lax.axis_index("narrow") * rows_part
    return unpack(place, limit, returned, (own_count, rows_part, BLK))


def solution(mesh):
    placed = (
        P("wide", None, "narrow"),
        P("wide", None, None),
        P("wide", "narrow"),
        P("wide", "narrow"),
        P("wide"),
    )
    return jax.shard_map(
        local, mesh=mesh, in_specs=placed, out_specs=P("wide", "narrow", None), check_vma=False
    )
```

```python
import jax
import jax.numpy as jnp
from jax import lax
from jax.experimental import pallas as pl
from jax.experimental.pallas import tpu as pltpu
from jax.sharding import PartitionSpec as P

CH = 12
L = 300
BLK = 128
EPS = 1e-06
CAP = 4
UNIT = 32
PLANE = 8
X, Y = 4, 2
PLANE_STEPS = ((0, 0), (1, 0), (3, 0), (0, 1), (2, 0), (1, 1), (3, 1), (2, 1))
CALLS = ((3, 6), (5, 2), (7, 4), (0, 1))
SHIFTS = 16
GROUP = 16
VMEM_LIMIT = 24 * 1024 * 1024
NT = (((1,), (1,)), ((), ()))
TN = (((0,), (0,)), ((), ()))


def lanes_of(shape):
    return lax.broadcasted_iota(jnp.int32, shape, len(shape) - 1)


def rows_of(shape):
    return lax.broadcasted_iota(jnp.int32, shape, len(shape) - 2)


def to_bf16(values):
    return values.astype(jnp.bfloat16)


def to_f32(values):
    return values.astype(jnp.float32)


def read_scalars(rows, weights, staged, scalars, sem):
    lane = lanes_of((8, 128))
    picked = jnp.zeros((8, 128), jnp.float32)
    for place, weight in weights:
        picked = jnp.where(lane == place, float(weight), picked)
    values = lax.dot_general(to_bf16(picked), rows, NT, preferred_element_type=jnp.float32)
    staged[...] = values.astype(jnp.int32)
    copy = pltpu.make_async_copy(staged, scalars, sem)
    copy.start()
    return copy


def pack_kernel(station_ref, block_ref, templates_ref, sent_ref, place_ref, padded, units, table, used):
    channels, templates, _ = templates_ref.shape
    rows_part = station_ref.shape[1]
    values = to_f32(templates_ref[...])
    centred = values - jnp.sum(values, axis=2, keepdims=True) / L
    power = jnp.sum(centred * centred, axis=2, keepdims=True) / L
    factor = 1.0 / (60.0 * jnp.sqrt(power + EPS))
    padded[...] = jnp.zeros_like(padded)
    padded[:, :, 0:L] = to_f32(to_bf16(centred))
    high = to_f32(to_bf16(factor))
    middle = to_f32(to_bf16(factor - high))
    low = to_f32(to_bf16(factor - high - middle))
    lane = lanes_of((templates, 128))
    marks = jnp.zeros((templates, 128), jnp.float32)
    for c in range(channels):
        marks = jnp.where(lane == c, high[c], marks)
        marks = jnp.where(lane == c + 16, middle[c], marks)
        marks = jnp.where(lane == c + 32, low[c], marks)
        units[:, c, :] = padded[c, :, 0:128]
        units[:, 12 + c, :] = padded[c, :, 128:256]
    for c in range(6):
        units[:, 24 + c, :] = padded[c, :, 256:384] + pltpu.roll(padded[c + 6, :, 256:384], 64, 1)
    units[:, 30, :] = marks
    units[:, 31, :] = jnp.zeros_like(marks)
    for z in range(sent_ref.shape[0]):
        sent_ref[z, 0:templates] = to_bf16(units[...])
    table[...] = jnp.zeros_like(table)

    def clear(h, carry):
        used[h] = 0
        return carry

    lax.fori_loop(0, used.shape[0], clear, 0, unroll=8)
    lane = lanes_of((1, 128))

    def place(k, r):
        station = station_ref[k, r]
        block = block_ref[k, r] & 31
        holder = station >> 3
        rank = jnp.minimum(used[holder], CAP - 1)
        used[holder] = rank + 1
        slot = holder * CAP + rank
        place_ref[k * rows_part + r] = slot
        entry = jnp.where(lane == 0, k, jnp.where(lane == 48, station & 7, jnp.where(lane == 49, block, 0)))
        table[pl.ds(slot, 1), :] = to_f32(entry)

    for k in range(templates):
        for r in range(rows_part):
            place(k, r)
    for z in range(sent_ref.shape[0]):
        sent_ref[z, templates] = to_bf16(table[UNIT * z : UNIT * z + UNIT, :])


def pack(station, block, templates, holders):
    channels, count, _ = templates.shape
    smem = pl.BlockSpec(memory_space=pltpu.SMEM)
    vmem = pl.BlockSpec(memory_space=pltpu.VMEM)
    return pl.pallas_call(
        pack_kernel,
        out_shape=(
            jax.ShapeDtypeStruct((holders // PLANE, count + 1, UNIT, 128), jnp.bfloat16),
            jax.ShapeDtypeStruct((count * station.shape[1],), jnp.int32),
        ),
        in_specs=[smem, smem, vmem],
        out_specs=(vmem, smem),
        scratch_shapes=[
            pltpu.VMEM((channels, count, 384), jnp.float32),
            pltpu.VMEM((count, UNIT, 128), jnp.float32),
            pltpu.VMEM((holders * CAP, 128), jnp.float32),
            pltpu.SMEM((holders,), jnp.int32),
        ],
        compiler_params=pltpu.CompilerParams(vmem_limit_bytes=60 * 1024 * 1024),
    )(station, block, templates)


def member_after(member, step):
    return (member // Y + step[0]) % X * Y + (member % Y + step[1]) % Y


def route_kernel(held_ref, ready_ref, *refs):
    sources = held_ref.shape[0]
    sent_refs, (tables, staged, chosen_ref, sem) = refs[:PLANE], refs[PLANE:]
    me = lax.axis_index("wide") % PLANE
    last = held_ref.shape[1] - 1
    tables[...] = to_f32(held_ref[:, last])
    entries = jnp.concatenate([held_ref[source, last] for source in range(sources)], axis=0)
    read_scalars(entries, ((0, 1),), staged, chosen_ref, sem).wait()
    lane, row = lanes_of((16, 128)), rows_of((16, 128))
    marked = (row == 14) & (lane >= 48) & (lane < 50)
    for step, sent_ref in zip(PLANE_STEPS, sent_refs):
        first = member_after(me, step) * CAP
        for source in range(sources):
            for j in range(CAP):
                chosen = chosen_ref[0, source * UNIT + first + j]
                slot = source * CAP + j
                sent_ref[slot, 0:16, :] = held_ref[source, chosen, 0:16, :]
                upper = to_f32(held_ref[source, chosen, 16:32, :])
                entry = jnp.broadcast_to(tables[source, pl.ds(first + j, 1), :], (16, 128))
                sent_ref[slot, 16:32, :] = to_bf16(jnp.where(marked, entry, upper))


def route(held, ready):
    sources = held.shape[0]
    vmem = pl.BlockSpec(memory_space=pltpu.VMEM)
    return pl.pallas_call(
        route_kernel,
        out_shape=[jax.ShapeDtypeStruct((sources * CAP, UNIT, 128), jnp.bfloat16)] * PLANE,
        in_specs=[vmem, pl.BlockSpec(memory_space=pl.ANY)],
        out_specs=[vmem] * PLANE,
        scratch_shapes=[
            pltpu.VMEM((sources, UNIT, 128), jnp.float32),
            pltpu.VMEM((8, sources * UNIT), jnp.int32),
            pltpu.SMEM((8, sources * UNIT), jnp.int32),
            pltpu.SemaphoreType.DMA,
        ],
        compiler_params=pltpu.CompilerParams(vmem_limit_bytes=VMEM_LIMIT),
        cost_estimate=pl.CostEstimate(flops=10_000_000_000, bytes_accessed=40_000_000, transcendentals=0),
    )(held, ready)


def station_kernel(wave_ref, tail_ref, shifted_ref, inverse_ref, signal, stacked):
    segment = wave_ref.shape[2]
    blocks = inverse_ref.shape[1]
    pieces = shifted_ref.shape[1]
    signal[CH:16, :] = jnp.zeros_like(signal[CH:16, :])
    signal[0:CH, 0:segment] = to_f32(wave_ref[0])
    signal[0:CH, segment:] = to_f32(tail_ref[0])
    lane, row = lanes_of((SHIFTS, 128)), rows_of((SHIFTS, 128))
    source = (lane + 8 * row) & 127
    inside = lane + 8 * row < 128

    for c in range(CH):
        before = None
        for piece in range(pieces + 1):
            here = jnp.broadcast_to(signal[c : c + 1, 128 * piece : 128 * piece + 128], (SHIFTS, 128))
            here = jnp.take_along_axis(here, source, axis=1)
            if piece > 0:
                shifted_ref[0, piece - 1, c] = to_bf16(jnp.where(inside, before, here))
            before = here
    for b in range(blocks):
        stacked[16 * b : 16 * b + 16, :] = signal[:, 128 * b : 128 * b + 512]
    sample, position = rows_of((512, 128)), lanes_of((512, 128))
    band = to_bf16(jnp.where((sample >= position) & (sample < position + L), 1.0, 0.0))
    values = stacked[...]
    squares = values * values
    high = to_bf16(squares)
    low = to_bf16(squares - to_f32(high))
    first = jnp.dot(to_bf16(values), band, preferred_element_type=jnp.float32) / L
    second = (
        jnp.dot(high, band, preferred_element_type=jnp.float32)
        + jnp.dot(low, band, preferred_element_type=jnp.float32)
    ) / L
    inverse = 1.0 / jnp.sqrt(second - first * first + EPS)
    inverse_ref[0] = inverse.reshape(blocks, 16, 128)


def station_tables(wave, tail):
    stations, channels, segment = wave.shape
    blocks = segment // BLK
    extra = tail.shape[2]
    return pl.pallas_call(
        station_kernel,
        grid=(stations,),
        out_shape=(
            jax.ShapeDtypeStruct((stations, blocks + 2, channels, SHIFTS, 128), jnp.bfloat16),
            jax.ShapeDtypeStruct((stations, blocks, 16, 128), jnp.float32),
        ),
        in_specs=[
            pl.BlockSpec((1, channels, segment), lambda s: (s, 0, 0)),
            pl.BlockSpec((1, channels, extra), lambda s: (s, 0, 0)),
        ],
        out_specs=(
            pl.BlockSpec((1, blocks + 2, channels, SHIFTS, 128), lambda s: (s, 0, 0, 0, 0)),
            pl.BlockSpec((1, blocks, 16, 128), lambda s: (s, 0, 0, 0)),
        ),
        scratch_shapes=[
            pltpu.VMEM((16, segment + extra), jnp.float32),
            pltpu.VMEM((16 * blocks, 512), jnp.float32),
        ],
        compiler_params=pltpu.CompilerParams(vmem_limit_bytes=VMEM_LIMIT),
        cost_estimate=pl.CostEstimate(flops=3_000_000_000, bytes_accessed=20_000_000, transcendentals=500_000),
    )(wave, tail)


def score_kernel(
    first_ref, second_ref, shifted_ref, inverse_ref, scores_ref, rows, marked, staged, codes, sem
):
    lane, row = lanes_of((8, 128)), rows_of((8, 128))
    before = lane < row
    member = lane // SHIFTS
    inverse_source = 8 * (lane % SHIFTS) + row
    natural_source = SHIFTS * row + lane // 8
    expand = to_bf16(jnp.where(lanes_of((GROUP, 256)) // SHIFTS == rows_of((GROUP, 256)), 1.0, 0.0))
    count = first_ref.shape[0]
    for start, units_ref in ((0, first_ref), (count, second_ref)):
        marked[start : start + count] = units_ref[:, 30, :]
    copy = read_scalars(marked[...], ((48, 32), (49, 1)), staged, codes, sem)
    for start, units_ref in ((0, first_ref), (count, second_ref)):
        units = units_ref[...]
        third = to_f32(units[:, 16:32, :])[:, 8:16, :]
        low_half = lanes_of(third.shape) < 64
        rows[start : start + count, 0:24, :] = to_f32(units)[:, 0:24, :]
        rows[start : start + count, 24:32, :] = jnp.where(low_half, third, 0.0)
        rows[start : start + count, 32:40, :] = jnp.where(low_half, pltpu.roll(third, 64, 2), 0.0)
    copy.wait()

    def template_rows(g, c):
        turned = []
        for r in (c, 12 + c, 24 + c if c < 6 else 26 + c):
            part = jnp.broadcast_to(rows[g, r : r + 1, :], (8, 128))
            turned.append(pltpu.roll(part, 0, 1, stride=1, stride_axis=0))
        return [
            jnp.where(before, 0.0, turned[0]),
            jnp.where(before, turned[0], turned[1]),
            jnp.where(before, turned[1], turned[2]),
        ]

    def score(group, carry):
        base = pl.multiple_of(group * GROUP, GROUP)
        marks = marked[pl.ds(base, GROUP), :]
        spread = lax.dot_general(marks, expand, TN, preferred_element_type=jnp.float32)
        factors = spread[0:12] + spread[16:28] + spread[32:44]
        totals = [jnp.zeros((8, 128), jnp.float32) for _ in range(2)]
        places = [(codes[0, base + g] >> 5, codes[0, base + g] & 31) for g in range(GROUP)]
        for c in range(CH):
            pairs = []
            for pair in range(GROUP // 2):
                one, two = template_rows(base + 2 * pair, c), template_rows(base + 2 * pair + 1, c)
                both = [to_bf16(jnp.concatenate([one[a], two[a]], axis=0)) for a in range(3)]
                pairs.append(jnp.concatenate(both, axis=1))
            products = lax.dot_general(
                jnp.concatenate(pairs, axis=0),
                jnp.concatenate(
                    [
                        jnp.concatenate([shifted_ref[s, b + a, c] for s, b in places], axis=0)
                        for a in range(3)
                    ],
                    axis=1,
                ),
                NT,
                preferred_element_type=jnp.float32,
            )
            for half in range(2):
                chosen = jnp.zeros((8, 128), jnp.float32)
                scale = jnp.zeros((8, 128), jnp.float32)
                for m in range(8):
                    g = 8 * half + m
                    station, block = places[g]
                    inverse = jnp.broadcast_to(inverse_ref[station, block, c : c + 1, :], (8, 128))
                    inverse = jnp.take_along_axis(inverse, inverse_source, axis=1)
                    mine = products[8 * g : 8 * g + 8, 128 * half : 128 * half + 128]
                    chosen = jnp.where(member == m, mine, chosen)
                    scale = jnp.where(member == m, inverse, scale)
                factor = factors[c : c + 1, 128 * half : 128 * half + 128]
                totals[half] = totals[half] + chosen * scale * factor
        for half in range(2):
            natural = jnp.zeros((8, 128), jnp.float32)
            for i in range(8):
                spread_row = jnp.broadcast_to(totals[half][i : i + 1], (8, 128))
                spread_row = jnp.take_along_axis(spread_row, natural_source, axis=1)
                natural = jnp.where(lane % 8 == i, spread_row, natural)
            for o in range(2):
                scores_ref[group * 4 + half * 2 + o] = natural[4 * o : 4 * o + 4]
        return carry

    lax.fori_loop(0, 2 * count // GROUP, score, 0)


def slot_scores(first, second, shifted, inverse):
    slots = 2 * first.shape[0]
    vmem = pl.BlockSpec(memory_space=pltpu.VMEM)
    return pl.pallas_call(
        score_kernel,
        out_shape=jax.ShapeDtypeStruct((slots // CAP, CAP, BLK), jnp.float32),
        in_specs=[vmem] * 4,
        out_specs=vmem,
        scratch_shapes=[
            pltpu.VMEM((slots, 40, 128), jnp.float32),
            pltpu.VMEM((slots, 128), jnp.bfloat16),
            pltpu.VMEM((8, slots), jnp.int32),
            pltpu.SMEM((8, slots), jnp.int32),
            pltpu.SemaphoreType.DMA,
        ],
        compiler_params=pltpu.CompilerParams(vmem_limit_bytes=VMEM_LIMIT),
        cost_estimate=pl.CostEstimate(flops=4_000_000_000, bytes_accessed=4_000_000, transcendentals=0),
    )(first, second, shifted, inverse)


def arrange_kernel(*refs):
    scores_refs, out_ref = refs[:-1], refs[-1]
    me = lax.axis_index("wide") % PLANE
    planes = out_ref.shape[0] // PLANE
    for scores_ref, pair in zip(scores_refs, CALLS):
        for place, number in enumerate(pair):
            step = PLANE_STEPS[number]
            member = member_after(me, (X - step[0], Y - step[1]))
            for z in range(planes):
                out_ref[z * PLANE + member] = scores_ref[place * planes + z]


def arrange(scores):
    vmem = pl.BlockSpec(memory_space=pltpu.VMEM)
    return pl.pallas_call(
        arrange_kernel,
        out_shape=jax.ShapeDtypeStruct((len(scores) * scores[0].shape[0], CAP, BLK), jnp.float32),
        in_specs=[vmem] * len(scores),
        out_specs=vmem,
        compiler_params=pltpu.CompilerParams(vmem_limit_bytes=VMEM_LIMIT),
    )(*scores)


def unpack_kernel(place_ref, limit_ref, scores_ref, out_ref):
    templates, rows_part, _ = out_ref.shape
    for k in range(templates):
        for r in range(rows_part):
            slot = place_ref[k * rows_part + r]
            found = scores_ref[slot >> 2, pl.ds(slot & 3, 1), :]
            out_ref[k, r : r + 1, :] = jnp.where(r < limit_ref[k], found, 0.0)


def unpack(place, limit, scores, shape):
    smem = pl.BlockSpec(memory_space=pltpu.SMEM)
    vmem = pl.BlockSpec(memory_space=pltpu.VMEM)
    return pl.pallas_call(
        unpack_kernel,
        out_shape=jax.ShapeDtypeStruct(shape, jnp.float32),
        in_specs=[smem, smem, vmem],
        out_specs=vmem,
        compiler_params=pltpu.CompilerParams(vmem_limit_bytes=VMEM_LIMIT),
    )(place, limit, scores)


def local(waveforms, templates, det_station, det_block, det_count):
    own_count, rows_part = det_station.shape
    wide_count = lax.axis_size("wide")
    narrow_count = lax.axis_size("narrow")
    planes = wide_count // PLANE
    members = [(z, p) for z in range(planes) for p in range(PLANE)]
    sent, place = pack(det_station, det_block, jnp.transpose(templates, (1, 0, 2)), wide_count)
    held = lax.all_to_all(
        sent.reshape(planes, (own_count + 1) * UNIT, 128),
        "wide",
        split_axis=0,
        concat_axis=0,
        tiled=True,
        axis_index_groups=[[PLANE * z + p for z in range(planes)] for p in range(PLANE)],
    )
    held = held.reshape(planes, own_count + 1, UNIT, 128)
    tail = lax.ppermute(
        waveforms[:, :, : 3 * BLK], "narrow", [(i, i - 1) for i in range(1, narrow_count)]
    )
    shifted, inverse = station_tables(waveforms, tail)
    routed = route(held, inverse)
    arrived = []
    for step, units in zip(PLANE_STEPS, routed):
        if step != (0, 0):
            pairs = [(PLANE * z + p, PLANE * z + member_after(p, step)) for z, p in members]
            units = lax.ppermute(units, "wide", pairs)
        arrived.append(units)
    scores = [slot_scores(arrived[a], arrived[b], shifted, inverse) for a, b in CALLS]
    returned = lax.all_to_all(arrange(scores), "wide", split_axis=0, concat_axis=0, tiled=True)
    limit = det_count - lax.axis_index("narrow") * rows_part
    return unpack(place, limit, returned, (own_count, rows_part, BLK))


def solution(mesh):
    placed = (
        P("wide", None, "narrow"),
        P("wide", None, None),
        P("wide", "narrow"),
        P("wide", "narrow"),
        P("wide"),
    )
    return jax.shard_map(
        local, mesh=mesh, in_specs=placed, out_specs=P("wide", "narrow", None), check_vma=False
    )
```
